128 devices in a mesh: dp: 2 (over core), pipe: 4 (over z), expert: 16 (over y, x).
Axes of the slice: x: 4, y: 4, z: 4, core: 2. Of those that a mesh axis runs over, the one named last changes fastest.
Arguments:
- out_grad: bfloat16 [4, 4096, 2560], P('pipe', ('dp', 'expert')), may hold values from -6 to 6
- routes: int32 [4, 4096, 6], P('pipe', ('dp', 'expert')), may hold values from 0 to 15, all different within a row; in each aligned block of 128 rows (0 to 127, 128 to 255, ..., all dimensions but the last counted through in order) at most 64 rows name the same one
- combine: bfloat16 [4, 4096, 6], P('pipe', ('dp', 'expert')), may hold values from 0.049804688 to 0.5
- gate_up_weight: bfloat16 [4, 16, 2560, 1792], P('pipe', 'expert', 'dp'), may hold values from -0.125 to 0.125
- down_weight: bfloat16 [4, 16, 896, 2560], P('pipe', 'expert', None, 'dp'), may hold values from -0.1875 to 0.1875
- saved_inputs: bfloat16 [4, 2, 16, 1024, 2560], P('pipe', 'dp', 'expert'), may hold values from -6 to 6
- saved_gate_up: bfloat16 [4, 2, 16, 1024, 1792], P('pipe', 'dp', 'expert'), may hold values from -6 to 6
Outputs:
- passed_grad: bfloat16 [4, 4096, 2560], P('pipe', ('dp', 'expert'))
- combine_grad: bfloat16 [4, 4096, 6], P('pipe', ('dp', 'expert'))
- gate_up_grad: bfloat16 [4, 16, 2560, 1792], P('pipe', 'expert', 'dp')
- down_grad: bfloat16 [4, 16, 896, 2560], P('pipe', 'expert', None, 'dp')
The draws below stay inside these ranges and needn't reach their ends.
Inputs may be any that keep to these rules, and one draw needn't show every extreme that they name: `routes`: the 6 numbers of a row differ. In each aligned block of 128 rows of a section no expert is named by more than 64 rows, and some block of every draw names some expert exactly 64 times.
All inputs are finite; a program needn't handle non-finite values.
Results may differ from the reference program's by a relative error of at most 0.0059.
Values may be sent and summed in bfloat16 or wider, within the bound.
A program may use at most 192 MiB of HBM per device.

```python
import math
import jax
import jax.numpy as jnp
import numpy as np
from jax import lax

D = 2560
FF = 896
EXPERTS = 16
TOP = 6
TOK_DEV = 128
SLOT = 64
ROWS = 1024
SECTIONS = 4
REPL = 2
TOKENS = 4096
N_EXPERT = 16


def level_of(key, dims, pieces, least, largest):
    factor_of, own = 1.0, jax.random.fold_in(key, 6)
    for dim, parts in pieces:
        steps = jnp.exp(jax.random.uniform(jax.random.fold_in(own, dim), (parts,), jnp.float32, least / len(pieces), largest / len(pieces)))
        factor_of = factor_of * jnp.repeat(steps, dims[dim] // parts).reshape([-1 if axis == dim else 1 for axis in range(len(dims))])
    return factor_of


def deal_out(stream_key, own, number, rows, amount, top, reach, lean):
    order = jax.random.permutation(stream_key, amount)
    crowded, usual = shares(amount, rows * top, reach, lean, True), shares(amount, rows * top, reach, lean, False)
    places = jnp.arange(amount)

    def named(sizes, offset_by):
        used = int((sizes > 0).sum())
        fixed = max(1, used // 4)
        moved = fixed + (places - fixed + offset_by * (used - fixed)) % max(1, amount - fixed)
        return jnp.zeros((amount,), jnp.int32).at[order[jnp.where(places < fixed, places, moved)]].set(jnp.asarray(sizes, jnp.int32))

    sizes = jnp.where(number % 4 == 0, named(crowded, number // 4), named(usual, number - number // 4 - 1))
    mixed = jax.random.permutation(jax.random.fold_in(own, 3), amount)
    giver, taker = mixed[0:amount // 2 * 2:2], mixed[1:amount // 2 * 2:2]
    margin = jnp.minimum(sizes[giver] - 1, reach - sizes[taker]) // 2
    margin = jnp.where((giver == order[0]) | (taker == order[0]) | (sizes[taker] == 0), 0, jnp.maximum(margin, 0))
    moved = jax.random.randint(jax.random.fold_in(own, 4), (amount // 2,), 0, 1 << 20) % (margin + 1)
    sizes = sizes.at[giver].add(-moved).at[taker].add(moved)
    members = jnp.searchsorted(jnp.cumsum(sizes), jnp.arange(rows * top), side="right").astype(jnp.int32)
    listing = members.reshape(top, rows).T
    listing = listing[jax.random.permutation(jax.random.fold_in(own, 1), rows)]
    offset_by = jax.random.randint(jax.random.fold_in(own, 2), (rows, 1), 0, top)
    return jnp.take_along_axis(listing, (jnp.arange(top)[None, :] + offset_by) % top, axis=1)


def shares(amount, total, limit, skew, full):
    loads = [(1 << 20) // math.isqrt(rank ** skew) + 1 for rank in range(1, amount + 1)]
    largest = limit if full else min(limit, max(-(-total // amount), total * loads[0] // sum(loads)))
    least = 1 if total - largest >= amount - 1 else 0
    given, spare = [largest] + [least] * (amount - 1), total - largest - least * (amount - 1)
    while spare > 0:
        free = [i for i in range(1, amount) if given[i] < largest] or [i for i in range(1, amount) if given[i] < limit]
        whole, remaining = sum([loads[i] for i in free]), spare
        for i in free:
            extra = min(limit - given[i], max(1, remaining * loads[i] // whole), spare)
            given[i] = given[i] + extra
            spare = spare - extra
    return np.array(given)


def noise(key, dims, deviation, bound, pieces=(), kind=jnp.bfloat16):
    array = deviation * jax.random.normal(key, dims, jnp.float32)
    if pieces:
        array = array * level_of(key, dims, pieces, -0.22, 0.18)
    return jnp.clip(array, -bound, bound).astype(kind)


def setup_inputs(seed: int = 0) -> dict:
    streams_of = jax.random.split(jax.random.key(seed), 8)
    out_grad = noise(streams_of[0], (SECTIONS, TOKENS, D), 1.0, 6.0, ((0, 4), (1, 32)))
    routes_keys = jax.random.split(jax.random.fold_in(streams_of[1], 1), SECTIONS * TOKENS // TOK_DEV)
    routes_turns = jax.random.permutation(jax.random.fold_in(streams_of[1], 3), SECTIONS * TOKENS // TOK_DEV)
    routes = jax.vmap(lambda own, number: deal_out(jax.random.fold_in(streams_of[1], 2), own, number, TOK_DEV, EXPERTS, TOP, SLOT, 2))(routes_keys, routes_turns).reshape((SECTIONS, TOKENS, TOP))
    combine = jnp.clip(jnp.exp(math.log(0.5) - 2.306499 * jax.random.uniform(streams_of[2], (SECTIONS, TOKENS, TOP), jnp.float32) ** level_of(streams_of[2], (SECTIONS, TOKENS, TOP), ((0, 4), (1, 32)), -0.2, 0.2)), 0.049804688, 0.5).astype(jnp.bfloat16)
    gate_up_weight = noise(streams_of[3], (SECTIONS, EXPERTS, D, 2 * FF), D ** -0.5, 0.125, ((0, 4), (1, 16), (2, 2)))
    down_weight = noise(streams_of[4], (SECTIONS, EXPERTS, FF, D), FF ** -0.5, 0.1875, ((0, 4), (1, 16), (3, 2)))
    saved_inputs = noise(streams_of[5], (SECTIONS, REPL, EXPERTS, ROWS, D), 1.0, 6.0, ((0, 4), (1, 2), (2, 16)))
    saved_gate_up = noise(streams_of[6], (SECTIONS, REPL, EXPERTS, ROWS, 2 * FF), 1.0, 6.0, ((0, 4), (1, 2), (2, 16)))
    return dict(out_grad=out_grad, routes=routes, combine=combine, gate_up_weight=gate_up_weight, down_weight=down_weight, saved_inputs=saved_inputs, saved_gate_up=saved_gate_up)


def slot_numbers(route_flat, experts):
    onehot = (route_flat[:, None] == jnp.arange(experts, dtype=jnp.int32)[None, :]).astype(jnp.int32)
    running = jnp.cumsum(onehot, axis=0)
    return (jnp.sum(running * onehot, axis=1) - 1).astype(jnp.int32)


def rounded(values):
    return lax.optimization_barrier(values.astype(jnp.bfloat16)).astype(jnp.float32)


def expert_rows(gu_rows, grad_rows, weight_rows, gate_up, down_proj):
    hidden_width = down_proj.shape[0]
    gate_pre = gu_rows[:, :hidden_width].astype(jnp.float32)
    up_pre = gu_rows[:, hidden_width:].astype(jnp.float32)
    logistic = jax.nn.sigmoid(gate_pre)
    activated = gate_pre * logistic
    hidden = activated * up_pre
    through = jnp.dot(grad_rows, down_proj.T, preferred_element_type=jnp.float32)
    comb_part = jnp.sum(through * hidden, axis=1).astype(jnp.bfloat16)
    factor = weight_rows.astype(jnp.float32)[:, None]
    scaled = (factor * hidden).astype(jnp.bfloat16)
    grad_hidden = factor * through
    grad_gate = grad_hidden * up_pre * logistic * (1.0 + gate_pre * (1.0 - logistic))
    grad_up = grad_hidden * activated
    grad_gu = jnp.concatenate([grad_gate, grad_up], axis=1).astype(jnp.bfloat16)
    input_grad = jnp.dot(grad_gu, gate_up.T, preferred_element_type=jnp.float32).astype(jnp.bfloat16)
    return input_grad, comb_part, grad_gu, scaled


def slots_of_source(route_row):
    return slot_numbers(route_row, EXPERTS)


def one_expert(operands):
    saved_x, saved_g, grad_rows, weight_rows, gate_up_one, down_one = operands
    input_grad, comb_part, grad_gu, scaled = expert_rows(saved_g, grad_rows, weight_rows, gate_up_one, down_one)
    part_gu = rounded(jnp.dot(saved_x.T, grad_gu, preferred_element_type=jnp.float32))
    part_down = rounded(jnp.dot(scaled.T, grad_rows, preferred_element_type=jnp.float32))
    return input_grad, comb_part, part_gu, part_down


def replica_pass(grad_tok, route_tok, comb_tok, saved_in, saved_gu, gate_up, down_proj):
    sources = N_EXPERT
    pair_count = TOK_DEV * TOP
    route_src = route_tok.reshape(sources, pair_count).astype(jnp.int32)
    slot_ids = jax.vmap(slots_of_source)(route_src)
    token_of = jnp.arange(pair_count, dtype=jnp.int32) // TOP
    source_of = jnp.broadcast_to(jnp.arange(sources, dtype=jnp.int32)[:, None], (sources, pair_count))
    grad_src = grad_tok.reshape(sources, TOK_DEV, D)
    picked = grad_src[source_of, token_of[None, :]]
    dispatched = jnp.zeros((EXPERTS, sources, SLOT, D), jnp.bfloat16).at[route_src, source_of, slot_ids].set(picked)
    weights = jnp.zeros((EXPERTS, sources, SLOT), jnp.bfloat16).at[route_src, source_of, slot_ids].set(comb_tok.reshape(sources, pair_count))
    mapped = lax.map(one_expert, (saved_in, saved_gu, dispatched.reshape(EXPERTS, ROWS, D), weights.reshape(EXPERTS, ROWS), gate_up, down_proj))
    returned = mapped[0].reshape(EXPERTS, sources, SLOT, D)[route_src, source_of, slot_ids]
    returned = returned.astype(jnp.float32).reshape(sources * TOK_DEV, TOP, D)
    layer_grad = jnp.sum(returned, axis=1).astype(jnp.bfloat16)
    comb_grad = mapped[1].reshape(EXPERTS, sources, SLOT)[route_src, source_of, slot_ids].reshape(sources * TOK_DEV, TOP)
    return layer_grad, comb_grad, mapped[2], mapped[3]


def reference(out_grad, routes, combine, gate_up_weight, down_weight, saved_inputs, saved_gate_up):
    group_rows = TOK_DEV * N_EXPERT
    layers = []
    comb_list = []
    gu_grads = []
    down_grads = []
    for section_no in range(SECTIONS):
        layer_parts = []
        comb_parts = []
        gu_total = jnp.zeros((EXPERTS, D, 2 * FF), jnp.float32)
        down_total = jnp.zeros((EXPERTS, FF, D), jnp.float32)
        for replica in range(REPL):
            first_row = replica * group_rows
            layer_grad, comb_grad, part_gu, part_down = replica_pass(
                out_grad[section_no, first_row:first_row + group_rows],
                routes[section_no, first_row:first_row + group_rows],
                combine[section_no, first_row:first_row + group_rows],
                saved_inputs[section_no, replica], saved_gate_up[section_no, replica],
                gate_up_weight[section_no], down_weight[section_no])
            layer_parts.append(layer_grad)
            comb_parts.append(comb_grad)
            gu_total = gu_total + part_gu
            down_total = down_total + part_down
        layers.append(jnp.concatenate(layer_parts, axis=0))
        comb_list.append(jnp.concatenate(comb_parts, axis=0))
        gu_grads.append(gu_total.astype(jnp.bfloat16))
        down_grads.append(down_total.astype(jnp.bfloat16))
    passed = jnp.roll(jnp.stack(layers), -1, axis=0)
    return passed, jnp.stack(comb_list), jnp.stack(gu_grads), jnp.stack(down_grads)
```

```python
import functools

import jax
import jax.numpy as jnp
from jax import lax
from jax.experimental import pallas as pl
from jax.experimental.pallas import tpu as pltpu
from jax.sharding import PartitionSpec as P

SLOT = 64
SIDE = 4
TOK = 128
EXPERTS = 16
MESH = pl.DeviceIdType.MESH
BF = jnp.bfloat16
F32 = jnp.float32
ORDER = (0, 1, 3, 2)


def mod4(i):
    return lax.rem(i, SIDE)


def at(half, u, v):
    return v * SIDE + u if half == 0 else u * SIDE + v


def remote(src, dst, send, recv, **where):
    return pltpu.make_async_remote_copy(
        src_ref=src, dst_ref=dst, send_sem=send, recv_sem=recv, device_id=where, device_id_type=MESH
    )


def enter(**peers):
    barrier = pltpu.get_barrier_semaphore()
    count = 0
    for axis, indices in peers.items():
        for index in indices:
            pl.semaphore_signal(barrier, inc=1, device_id={axis: index}, device_id_type=MESH)
            count += 1
    pl.semaphore_wait(barrier, count)


def one_hot(slots_row):
    ids = lax.broadcasted_iota(jnp.int32, (SLOT, TOK), 0).astype(F32)
    return jnp.where(ids == slots_row, 1.0, 0.0).astype(BF)


def dispatch_kernel(
    tok, routes, combine, wgu, wdn,
    dya, dyb, table, wgu_peer, wdn_peer,
    gathered, staged, relayed, send, recv, table_send, table_recv, dp_send, dp_recv,
):
    me = lax.axis_index("expert")
    dp = lax.axis_index("dp")
    y, x = lax.div(me, SIDE), lax.rem(me, SIDE)
    width = tok.shape[1] // 2
    outs = (dya, dyb)
    uv = ((x, y), (y, x))
    row_peers = [y * SIDE + mod4(x + i) for i in (1, 2, 3)]
    col_peers = [mod4(y + i) * SIDE + x for i in (1, 2, 3)]
    enter(expert=row_peers + col_peers, dp=[1 - dp])
    sends = []

    def go(copy):
        copy.start()
        sends.append(copy)
        return copy

    def ring(half, step):
        u, v = uv[half]
        up, down = at(half, mod4(u + 1), v), at(half, mod4(u + 3), v)
        if step == 0:
            mine = tok.at[:, pl.ds(half * width, width)]
            return (
                remote(mine, gathered.at[half, u], send.at[half, 0], recv.at[half, 0], expert=down),
                remote(mine, gathered.at[half, u], send.at[half, 1], recv.at[half, 1], expert=up),
            )
        first = gathered.at[half, mod4(u + 1), pl.ds(0, TOK // 2)]
        second = gathered.at[half, mod4(u + 3), pl.ds(TOK // 2, TOK // 2)]
        return (
            remote(first, first, send.at[half, 2], recv.at[half, 2], expert=down),
            remote(second, second, send.at[half, 3], recv.at[half, 3], expert=up),
        )

    near = [ring(half, 0) for half in (0, 1)]
    for half in (0, 1):
        for copy in near[half]:
            go(copy)

    ids = lax.broadcasted_iota(jnp.int32, (EXPERTS, TOK), 0)
    chosen = jnp.zeros((EXPERTS, TOK), F32)
    weight = jnp.zeros((EXPERTS, TOK), F32)
    for k in range(routes.shape[0]):
        hit = jnp.where(ids == routes[pl.ds(k, 1), :], 1.0, 0.0)
        chosen = chosen + hit
        weight = weight + hit * combine[pl.ds(k, 1), :]
    before = lax.broadcasted_iota(jnp.int32, (TOK, TOK), 0) < lax.broadcasted_iota(
        jnp.int32, (TOK, TOK), 1
    )
    count = jnp.dot(
        chosen.astype(BF), jnp.where(before, 1.0, 0.0).astype(BF), preferred_element_type=F32
    )
    slots = jnp.where(chosen > 0.5, count, -1.0)
    table[pl.ds(me, 1)] = jnp.concatenate([slots, weight], axis=0)[None]

    row_tables = [
        remote(
            table.at[me], table.at[me], table_send.at[i], table_recv.at[i], expert=row_peers[i]
        )
        for i in range(3)
    ]
    for copy in row_tables:
        go(copy)
    across = [
        remote(wgu, wgu_peer, dp_send.at[0], dp_recv.at[0], dp=1 - dp),
        remote(wdn, wdn_peer, dp_send.at[1], dp_recv.at[1], dp=1 - dp),
    ]
    for copy in across:
        go(copy)

    def deliver(half, r):
        u, v = uv[half]
        source_u = mod4(u + ORDER[r])
        source = at(half, source_u, v)
        maps = [
            one_hot(table[pl.ds(source, 1), pl.ds(at(half, u, mod4(v + j)), 1), :][0])
            for j in range(SIDE)
        ]
        if r == 0:
            block = tok[:, pl.ds(half * width, width)]
        else:
            block = gathered[pl.ds(half, 1), pl.ds(source_u, 1)][0, 0]
        rows = jnp.dot(jnp.concatenate(maps, axis=0), block, preferred_element_type=F32)
        staged[half, r] = rows.astype(BF).reshape(SIDE, SLOT, width)
        up, down = at(half, u, mod4(v + 1)), at(half, u, mod4(v + 3))
        low, high = pl.ds(0, SLOT // 2), pl.ds(SLOT // 2, SLOT // 2)
        out = outs[half]
        i = 12 + 2 * r
        go(remote(staged.at[half, r, 2, low], relayed.at[half, 0, r], send.at[half, i], recv.at[half, i], expert=up))
        go(remote(staged.at[half, r, 2, high], relayed.at[half, 1, r], send.at[half, i + 1], recv.at[half, i + 1], expert=down))
        i = 4 + 2 * r
        go(remote(staged.at[half, r, 1], out.at[source], send.at[half, i], recv.at[half, i], expert=up))
        go(remote(staged.at[half, r, 3], out.at[source], send.at[half, i + 1], recv.at[half, i + 1], expert=down))
        own = pltpu.make_async_copy(staged.at[half, r, 0], out.at[source], send.at[half, 28 + r])
        own.start()
        return own

    def forward(half, r):
        u, v = uv[half]
        source_u = mod4(u + ORDER[r])
        low, high = pl.ds(0, SLOT // 2), pl.ds(SLOT // 2, SLOT // 2)
        up, down = at(half, u, mod4(v + 1)), at(half, u, mod4(v + 3))
        out = outs[half]
        for d, to, part, origin in ((0, up, low, mod4(v + 3)), (1, down, high, mod4(v + 1))):
            slot = relayed.at[half, d, r]
            i = 12 + 2 * r + d
            remote(slot, slot, send.at[half, i], recv.at[half, i], expert=to).wait_recv()
            i = 20 + 2 * r + d
            go(remote(slot, out.at[at(half, source_u, origin), part], send.at[half, i], recv.at[half, i], expert=to))

    owns = [deliver(half, 0) for half in (0, 1)]
    for copy in row_tables:
        copy.wait_recv()
    mine = pl.ds(y * SIDE, SIDE)
    col_tables = [
        remote(
            table.at[mine], table.at[mine], table_send.at[3 + i], table_recv.at[3 + i], expert=col_peers[i]
        )
        for i in range(3)
    ]
    for copy in col_tables:
        go(copy)
    for half in (0, 1):
        for copy in near[half]:
            copy.wait_recv()
        for copy in ring(half, 1):
            go(copy)
    for copy in col_tables:
        copy.wait_recv()
    for r in (1, 2):
        for half in (0, 1):
            owns.append(deliver(half, r))
            forward(half, r - 1)
    for half in (0, 1):
        for copy in ring(half, 1):
            copy.wait_recv()
        owns.append(deliver(half, 3))
    for r in (2, 3):
        for half in (0, 1):
            forward(half, r)
    for half in (0, 1):
        for r in range(SIDE):
            for d in (0, 1):
                low = pl.ds(0, SLOT // 2)
                for i, piece in ((4 + 2 * r + d, outs[half].at[0]), (20 + 2 * r + d, outs[half].at[0, low])):
                    remote(piece, piece, send.at[half, i], recv.at[half, i], expert=me).wait_recv()
    for copy in owns:
        copy.wait()
    for copy in across:
        copy.wait_recv()
    for copy in sends:
        copy.wait_send()


def dispatch(tok, routes, combine, wgu, wdn):
    width = tok.shape[1] // 2
    vmem = pl.BlockSpec(memory_space=pltpu.VMEM)
    anyw = pl.BlockSpec(memory_space=pl.ANY)
    block = jax.ShapeDtypeStruct((EXPERTS, SLOT, width), BF)
    return pl.pallas_call(
        dispatch_kernel,
        out_shape=(
            block,
            block,
            jax.ShapeDtypeStruct((EXPERTS, 2 * EXPERTS, TOK), F32),
            jax.ShapeDtypeStruct(wgu.shape, BF),
            jax.ShapeDtypeStruct(wdn.shape, BF),
        ),
        in_specs=[vmem, vmem, vmem, anyw, anyw],
        out_specs=(anyw, anyw, vmem, anyw, anyw),
        scratch_shapes=[
            pltpu.VMEM((2, SIDE, TOK, width), BF),
            pltpu.VMEM((2, SIDE, SIDE, SLOT, width), BF),
            pltpu.VMEM((2, 2, SIDE, SLOT // 2, width), BF),
            pltpu.SemaphoreType.DMA((2, 32)),
            pltpu.SemaphoreType.DMA((2, 32)),
            pltpu.SemaphoreType.DMA((6,)),
            pltpu.SemaphoreType.DMA((6,)),
            pltpu.SemaphoreType.DMA((2,)),
            pltpu.SemaphoreType.DMA((2,)),
        ],
        compiler_params=pltpu.CompilerParams(
            collective_id=0, has_side_effects=True, vmem_limit_bytes=40 * 1024 * 1024
        ),
        name="dispatch",
    )(tok, routes, combine, wgu, wdn)


def rounded(values):
    return lax.optimization_barrier(values.astype(jnp.bfloat16)).astype(jnp.float32)


def shifted(block, axis, distance):
    devices = range(lax.axis_size(axis))
    route = [((i - distance) % len(devices), i) for i in devices]
    return lax.ppermute(block, axis, route)


def body(out_grad, routes, combine, gate_up_weight, down_weight, saved_inputs, saved_gate_up):
    me = lax.axis_index("expert")
    dp = lax.axis_index("dp")
    rt, cb = routes[0].T, combine[0].T.astype(F32)
    dya, dyb, table, wgu_peer, wdn_peer = dispatch(out_grad[0], rt, cb, gate_up_weight[0, 0], down_weight[0, 0])
    first = dp == 0
    own_gu, own_dn = gate_up_weight[0, 0], down_weight[0, 0]
    gate_up = jnp.concatenate([jnp.where(first, own_gu, wgu_peer), jnp.where(first, wgu_peer, own_gu)], axis=0)
    down_proj = jnp.concatenate([jnp.where(first, own_dn, wdn_peer), jnp.where(first, wdn_peer, own_dn)], axis=1)
    dy = jnp.concatenate([dya, dyb], axis=2).reshape(1024, -1)
    ids = jnp.arange(SLOT, dtype=F32)
    s_all, w_all = table[:, :EXPERTS], table[:, EXPERTS:]
    s_me = lax.dynamic_index_in_dim(s_all, me, 1, keepdims=False)
    w_me = lax.dynamic_index_in_dim(w_all, me, 1, keepdims=False)
    weight_rows = jnp.sum(jnp.where(ids[None, :, None] == s_me[:, None, :], w_me[:, None, :], 0.0), axis=2).reshape(-1)
    gu_rows = saved_gate_up[0, 0, 0]
    ff = gu_rows.shape[1] // 2
    gate_pre = gu_rows[:, :ff].astype(F32)
    up_pre = gu_rows[:, ff:].astype(F32)
    logistic = jax.nn.sigmoid(gate_pre)
    activated = gate_pre * logistic
    hidden = activated * up_pre
    through = lax.dot_general(dy, down_proj, (((1,), (1,)), ((), ())), preferred_element_type=F32)
    comb_part = jnp.sum(through * hidden, axis=1).astype(BF)
    factor = weight_rows[:, None]
    scaled = (factor * hidden).astype(BF)
    grad_hidden = factor * through
    grad_gate = grad_hidden * up_pre * logistic * (1.0 + gate_pre * (1.0 - logistic))
    grad_up = grad_hidden * activated
    grad_gu = jnp.concatenate([grad_gate, grad_up], axis=1).astype(BF)
    input_grad = lax.dot_general(grad_gu, gate_up, (((1,), (1,)), ((), ())), preferred_element_type=F32).astype(BF)
    back = lax.all_to_all(input_grad.reshape(1, 16, SLOT, -1), "expert", split_axis=1, concat_axis=1, tiled=True)
    comb = lax.all_to_all(comb_part.reshape(1, 16, SLOT), "expert", split_axis=1, concat_axis=1, tiled=True)[0]
    s_own = lax.dynamic_index_in_dim(s_all, me, 0, keepdims=False)
    onehot = (ids[None, :, None] == s_own[:, None, :]).astype(BF).reshape(1024, TOK)
    layer = lax.dot_general(onehot, back.reshape(1024, -1), (((0,), (0,)), ((), ())), preferred_element_type=F32).astype(BF)
    passed = shifted(layer[None], "pipe", -1)
    comb_et = jnp.sum(onehot.reshape(16, SLOT, TOK).astype(F32) * comb[:, :, None].astype(F32), axis=1)
    comb_grad = jnp.sum(jnp.where(rt[:, None, :] == jnp.arange(16)[None, :, None], comb_et[None], 0.0), axis=1).T.astype(BF)[None]
    part_gu = jnp.einsum("rd,rf->df", saved_inputs[0, 0, 0], grad_gu, preferred_element_type=F32).astype(BF)
    part_dn = jnp.einsum("rf,rd->fd", scaled, dy, preferred_element_type=F32).astype(BF)
    sum_gu = lax.psum_scatter(part_gu, "dp", scatter_dimension=0, tiled=True)
    sum_dn = lax.psum_scatter(part_dn, "dp", scatter_dimension=1, tiled=True)
    return passed, comb_grad, sum_gu[None, None], sum_dn[None, None]


def solution(mesh):
    placed = (
        P("pipe", ("dp", "expert"), None),
        P("pipe", ("dp", "expert"), None),
        P("pipe", ("dp", "expert"), None),
        P("pipe", "expert", "dp", None),
        P("pipe", "expert", None, "dp"),
        P("pipe", "dp", "expert", None, None),
        P("pipe", "dp", "expert", None, None),
    )
    return jax.shard_map(
        body,
        mesh=mesh,
        in_specs=placed,
        out_specs=(
            P("pipe", ("dp", "expert"), None),
            P("pipe", ("dp", "expert"), None),
            P("pipe", "expert", "dp", None),
            P("pipe", "expert", None, "dp"),
        ),
        check_vma=False,
    )
```

```python
import functools

import jax
import jax.numpy as jnp
from jax import lax
from jax.experimental import pallas as pl
from jax.experimental.pallas import tpu as pltpu
from jax.sharding import PartitionSpec as P

SLOT = 64
SIDE = 4
TOK = 128
EXPERTS = 16
MESH = pl.DeviceIdType.MESH
BF = jnp.bfloat16
F32 = jnp.float32
ORDER = (0, 1, 3, 2)
CHUNKS = ((0, 768), (768, 512))
DN_CUTS = ((0, 384), (384, 512))


def mod4(i):
    return lax.rem(i, SIDE)


def at(half, u, v):
    return v * SIDE + u if half == 0 else u * SIDE + v


def remote(src, dst, send, recv, **where):
    return pltpu.make_async_remote_copy(
        src_ref=src, dst_ref=dst, send_sem=send, recv_sem=recv, device_id=where, device_id_type=MESH
    )


def enter(**peers):
    barrier = pltpu.get_barrier_semaphore()
    count = 0
    for axis, indices in peers.items():
        for index in indices:
            pl.semaphore_signal(barrier, inc=1, device_id={axis: index}, device_id_type=MESH)
            count += 1
    pl.semaphore_wait(barrier, count)


def one_hot(slots_row):
    ids = lax.broadcasted_iota(jnp.int32, (SLOT, TOK), 0).astype(F32)
    return jnp.where(ids == slots_row, 1.0, 0.0).astype(BF)


def dispatch_kernel(
    tok, routes, combine, wgu, wdn, saved,
    dya, dyb, table, wgu_peer, wdn_peer, coef_out, hidden_out, scaled_out,
    gathered, staged, relayed, held, coef, hidden, scaled,
    send, recv, table_send, table_recv, dp_send, dp_recv, load_sem, store_sem,
):
    me = lax.axis_index("expert")
    dp = lax.axis_index("dp")
    y, x = lax.div(me, SIDE), lax.rem(me, SIDE)
    width = tok.shape[1] // 2
    outs = (dya, dyb)
    uv = ((x, y), (y, x))
    row_peers = [y * SIDE + mod4(x + i) for i in (1, 2, 3)]
    col_peers = [mod4(y + i) * SIDE + x for i in (1, 2, 3)]
    load = pltpu.make_async_copy(saved, held, load_sem)
    load.start()
    enter(expert=row_peers + col_peers, dp=[1 - dp])
    sends = []

    def go(copy):
        copy.start()
        sends.append(copy)
        return copy

    def ring(half, step):
        u, v = uv[half]
        up, down = at(half, mod4(u + 1), v), at(half, mod4(u + 3), v)
        if step == 0:
            mine = tok.at[:, pl.ds(half * width, width)]
            return (
                remote(mine, gathered.at[half, u], send.at[half, 0], recv.at[half, 0], expert=down),
                remote(mine, gathered.at[half, u], send.at[half, 1], recv.at[half, 1], expert=up),
            )
        first = gathered.at[half, mod4(u + 1), pl.ds(0, TOK // 2)]
        second = gathered.at[half, mod4(u + 3), pl.ds(TOK // 2, TOK // 2)]
        return (
            remote(first, first, send.at[half, 2], recv.at[half, 2], expert=down),
            remote(second, second, send.at[half, 3], recv.at[half, 3], expert=up),
        )

    near = [ring(half, 0) for half in (0, 1)]
    for half in (0, 1):
        for copy in near[half]:
            go(copy)

    ids = lax.broadcasted_iota(jnp.int32, (EXPERTS, TOK), 0)
    chosen = jnp.zeros((EXPERTS, TOK), F32)
    weight = jnp.zeros((EXPERTS, TOK), F32)
    for k in range(routes.shape[0]):
        hit = jnp.where(ids == routes[pl.ds(k, 1), :], 1.0, 0.0)
        chosen = chosen + hit
        weight = weight + hit * combine[pl.ds(k, 1), :]
    before = lax.broadcasted_iota(jnp.int32, (TOK, TOK), 0) < lax.broadcasted_iota(
        jnp.int32, (TOK, TOK), 1
    )
    count = jnp.dot(
        chosen.astype(BF), jnp.where(before, 1.0, 0.0).astype(BF), preferred_element_type=F32
    )
    slots = jnp.where(chosen > 0.5, count, -1.0)
    table[pl.ds(me, 1)] = jnp.concatenate([slots, weight], axis=0)[None]

    row_tables = [
        remote(
            table.at[me], table.at[me], table_send.at[i], table_recv.at[i], expert=row_peers[i]
        )
        for i in range(3)
    ]
    for copy in row_tables:
        go(copy)
    across = [
        remote(wgu, wgu_peer, dp_send.at[0], dp_recv.at[0], dp=1 - dp),
        remote(wdn, wdn_peer, dp_send.at[1], dp_recv.at[1], dp=1 - dp),
    ]
    for copy in across:
        go(copy)

    def deliver(half, r):
        u, v = uv[half]
        source_u = mod4(u + ORDER[r])
        source = at(half, source_u, v)
        maps = [
            one_hot(table[pl.ds(source, 1), pl.ds(at(half, u, mod4(v + j)), 1), :][0])
            for j in range(SIDE)
        ]
        if r == 0:
            block = tok[:, pl.ds(half * width, width)]
        else:
            block = gathered[pl.ds(half, 1), pl.ds(source_u, 1)][0, 0]
        rows = jnp.dot(jnp.concatenate(maps, axis=0), block, preferred_element_type=F32)
        staged[half, r] = rows.astype(BF).reshape(SIDE, SLOT, width)
        up, down = at(half, u, mod4(v + 1)), at(half, u, mod4(v + 3))
        low, high = pl.ds(0, SLOT // 2), pl.ds(SLOT // 2, SLOT // 2)
        out = outs[half]
        i = 12 + 2 * r
        go(remote(staged.at[half, r, 2, low], relayed.at[half, 0, r], send.at[half, i], recv.at[half, i], expert=up))
        go(remote(staged.at[half, r, 2, high], relayed.at[half, 1, r], send.at[half, i + 1], recv.at[half, i + 1], expert=down))
        i = 4 + 2 * r
        go(remote(staged.at[half, r, 1], out.at[source], send.at[half, i], recv.at[half, i], expert=up))
        go(remote(staged.at[half, r, 3], out.at[source], send.at[half, i + 1], recv.at[half, i + 1], expert=down))
        own = pltpu.make_async_copy(staged.at[half, r, 0], out.at[source], send.at[half, 28 + r])
        own.start()
        return own

    def forward(half, r):
        u, v = uv[half]
        source_u = mod4(u + ORDER[r])
        low, high = pl.ds(0, SLOT // 2), pl.ds(SLOT // 2, SLOT // 2)
        up, down = at(half, u, mod4(v + 1)), at(half, u, mod4(v + 3))
        out = outs[half]
        for d, to, part, origin in ((0, up, low, mod4(v + 3)), (1, down, high, mod4(v + 1))):
            slot = relayed.at[half, d, r]
            i = 12 + 2 * r + d
            remote(slot, slot, send.at[half, i], recv.at[half, i], expert=to).wait_recv()
            i = 20 + 2 * r + d
            go(remote(slot, out.at[at(half, source_u, origin), part], send.at[half, i], recv.at[half, i], expert=to))

    ff = hidden.shape[1]
    stores = []

    def prepare(quarter):
        @pl.loop(0, SIDE)
        def _(i):
            source = quarter * SIDE + i
            rows = pl.ds(pl.multiple_of(source * SLOT, SLOT), SLOT)
            mine = table[pl.ds(source, 1), pl.ds(me, 1), :][0]
            given = table[pl.ds(source, 1), pl.ds(EXPERTS + me, 1), :][0]
            ids = lax.broadcasted_iota(jnp.int32, (SLOT, TOK), 0).astype(F32)
            factor = jnp.sum(jnp.where(ids == mine, given, 0.0), axis=1, keepdims=True)
            gate = held[rows, pl.ds(0, ff)].astype(F32)
            up = held[rows, pl.ds(ff, ff)].astype(F32)
            logistic = 1.0 / (1.0 + jnp.exp(-gate))
            active = gate * logistic
            value = active * up
            hidden[rows, :] = value
            scaled[rows, :] = (factor * value).astype(BF)
            slope = up * logistic * (1.0 + gate * (1.0 - logistic))
            coef[rows, pl.ds(0, ff)] = factor * slope
            coef[rows, pl.ds(ff, ff)] = factor * active

        rows = pl.ds(quarter * SIDE * SLOT, SIDE * SLOT)
        for i, (src, dst) in enumerate(((coef, coef_out), (hidden, hidden_out), (scaled, scaled_out))):
            copy = pltpu.make_async_copy(src.at[rows], dst.at[rows], store_sem.at[quarter, i])
            copy.start()
            stores.append(copy)

    owns = [deliver(half, 0) for half in (0, 1)]
    for copy in row_tables:
        copy.wait_recv()
    mine = pl.ds(y * SIDE, SIDE)
    col_tables = [
        remote(
            table.at[mine], table.at[mine], table_send.at[3 + i], table_recv.at[3 + i], expert=col_peers[i]
        )
        for i in range(3)
    ]
    for copy in col_tables:
        go(copy)
    for half in (0, 1):
        for copy in near[half]:
            copy.wait_recv()
        for copy in ring(half, 1):
            go(copy)
    for copy in col_tables:
        copy.wait_recv()
    for r in (1, 2):
        for half in (0, 1):
            owns.append(deliver(half, r))
            forward(half, r - 1)
    for half in (0, 1):
        for copy in ring(half, 1):
            copy.wait_recv()
        owns.append(deliver(half, 3))
    load.wait()
    prepare(0)
    for half in (0, 1):
        forward(half, 2)
    for quarter in (1, 2, 3):
        prepare(quarter)
    for half in (0, 1):
        forward(half, 3)
    for half in (0, 1):
        for r in range(SIDE):
            for d in (0, 1):
                low = pl.ds(0, SLOT // 2)
                for i, piece in ((4 + 2 * r + d, outs[half].at[0]), (20 + 2 * r + d, outs[half].at[0, low])):
                    remote(piece, piece, send.at[half, i], recv.at[half, i], expert=me).wait_recv()
    for copy in owns + stores:
        copy.wait()
    for copy in across:
        copy.wait_recv()
    for copy in sends:
        copy.wait_send()


def dispatch(tok, routes, combine, wgu, wdn, saved):
    rows, both = saved.shape
    width = tok.shape[1] // 2
    vmem = pl.BlockSpec(memory_space=pltpu.VMEM)
    anyw = pl.BlockSpec(memory_space=pltpu.HBM)
    block = jax.ShapeDtypeStruct((EXPERTS, SLOT, width), BF)
    return pl.pallas_call(
        dispatch_kernel,
        out_shape=(
            block,
            block,
            jax.ShapeDtypeStruct((EXPERTS, 2 * EXPERTS, TOK), F32),
            jax.ShapeDtypeStruct(wgu.shape, BF),
            jax.ShapeDtypeStruct(wdn.shape, BF),
            jax.ShapeDtypeStruct((rows, both), F32),
            jax.ShapeDtypeStruct((rows, both // 2), F32),
            jax.ShapeDtypeStruct((rows, both // 2), BF),
        ),
        in_specs=[vmem, vmem, vmem, anyw, anyw, anyw],
        out_specs=(anyw, anyw, vmem, anyw, anyw, anyw, anyw, anyw),
        scratch_shapes=[
            pltpu.VMEM((2, SIDE, TOK, width), BF),
            pltpu.VMEM((2, SIDE, SIDE, SLOT, width), BF),
            pltpu.VMEM((2, 2, SIDE, SLOT // 2, width), BF),
            pltpu.VMEM((rows, both), BF),
            pltpu.VMEM((rows, both), F32),
            pltpu.VMEM((rows, both // 2), F32),
            pltpu.VMEM((rows, both // 2), BF),
            pltpu.SemaphoreType.DMA((2, 32)),
            pltpu.SemaphoreType.DMA((2, 32)),
            pltpu.SemaphoreType.DMA((6,)),
            pltpu.SemaphoreType.DMA((6,)),
            pltpu.SemaphoreType.DMA((2,)),
            pltpu.SemaphoreType.DMA((2,)),
            pltpu.SemaphoreType.DMA,
            pltpu.SemaphoreType.DMA((SIDE, 3)),
        ],
        compiler_params=pltpu.CompilerParams(
            collective_id=0, has_side_effects=True, vmem_limit_bytes=62 * 1024 * 1024
        ),
        name="dispatch",
    )(tok, routes, combine, wgu, wdn, saved)


def contract(a, b, da, db):
    return lax.dot_general(a, b, (((da,), (db,)), ((), ())), preferred_element_type=F32)


def backward_kernel(
    dya, dyb, table, wgu_own, wgu_peer, wdn_own, wdn_peer, coef_in, hidden_in, scaled_in, inputs,
    passed, comb_in, gu_own, gu_recv, dn_own, dn_recv,
    wgu, wdn, dy, saved, scaled, coef, hidden, grad,
    outgoing, returned, relayed, partial, sending, half_in, full_in, final,
    comb_out, comb_mid, gu_stage, dn_stage,
    load_sem, part_sem, send, recv, comb_send, comb_recv, dw_send, dw_recv, own_sem,
):
    me = lax.axis_index("expert")
    dp = lax.axis_index("dp")
    pipe = lax.axis_index("pipe")
    y, x = lax.div(me, SIDE), lax.rem(me, SIDE)
    width = dy.shape[-1]
    ff = hidden.shape[-1]
    uv = ((x, y), (y, x))
    row_peers = [y * SIDE + mod4(x + i) for i in (1, 2, 3)]
    col_peers = [mod4(y + i) * SIDE + x for i in (1, 2, 3)]
    chunks = CHUNKS
    group = SIDE * SLOT

    loads = {}

    def load(name, src, dst, sem):
        loads[name] = pltpu.make_async_copy(src, dst, sem)
        loads[name].start()

    def stream(q):
        rows = pl.ds(q * group, group)
        load(("coef", q), coef_in.at[rows], coef.at[q % 2], part_sem.at[q, 0])
        load(("hidden", q), hidden_in.at[rows], hidden.at[q % 2], part_sem.at[q, 1])

    load("wdn_own", wdn_own, wdn.at[dp], load_sem.at[0])
    load("wdn_peer", wdn_peer, wdn.at[1 - dp], load_sem.at[1])
    load("dya", dya, dy.at[0], load_sem.at[2])
    load("dyb", dyb, dy.at[1], load_sem.at[3])
    stream(0)
    stream(1)
    load("wgu_own", wgu_own, wgu.at[dp], load_sem.at[4])
    load("wgu_peer", wgu_peer, wgu.at[1 - dp], load_sem.at[5])
    load("scaled", scaled_in, scaled, load_sem.at[6])
    load("in0", inputs.at[:, pl.ds(0, width)], saved.at[0], load_sem.at[7])
    load("in1", inputs.at[:, pl.ds(width, width)], saved.at[1], load_sem.at[8])
    enter(
        expert=row_peers + col_peers,
        dp=[1 - dp],
        pipe=[mod4(pipe + 1), mod4(pipe + 3)],
    )
    sends = []

    def go(copy):
        copy.start()
        sends.append(copy)
        return copy

    for name in ("wdn_own", "wdn_peer", "dya", "dyb"):
        loads[name].wait()
    for q in range(SIDE):
        loads[("coef", q)].wait()
        loads[("hidden", q)].wait()
        sources = pl.ds(q * SIDE, SIDE)
        through = contract(dy[0, sources].reshape(group, width), wdn[0], 1, 1) + contract(
            dy[1, sources].reshape(group, width), wdn[1], 1, 1
        )
        comb = jnp.sum(through * hidden[q % 2], axis=1, keepdims=True).astype(BF).astype(F32)
        factor = coef[q % 2]
        grad[q, :, :, pl.ds(0, ff)] = (through * factor[:, :ff]).astype(BF).reshape(SIDE, SLOT, ff)
        grad[q, :, :, pl.ds(ff, ff)] = (through * factor[:, ff:]).astype(BF).reshape(SIDE, SLOT, ff)
        for i in range(SIDE):
            source = q * SIDE + i
            chosen = one_hot(table[source, pl.ds(me, 1), :]).astype(F32)
            row = jnp.sum(chosen * comb[i * SLOT : (i + 1) * SLOT], axis=0, keepdims=True)
            comb_out[source] = jnp.broadcast_to(row, comb_out.shape[1:])
        if q + 2 < SIDE:
            stream(q + 2)

    comb_mid[pl.ds(y, 1)] = comb_out[pl.ds(pl.multiple_of(y * SIDE, SIDE), SIDE)][None]
    comb_cols = [
        remote(
            comb_out.at[pl.ds(mod4(y + i) * SIDE, SIDE)], comb_mid.at[y],
            comb_send.at[i - 1], comb_recv.at[i - 1], expert=col_peers[i - 1],
        )
        for i in (1, 2, 3)
    ]
    comb_rows = [
        remote(
            comb_mid.at[:, mod4(x + i)], comb_in.at[x],
            comb_send.at[2 + i], comb_recv.at[2 + i], expert=row_peers[i - 1],
        )
        for i in (1, 2, 3)
    ]
    for copy in comb_cols:
        go(copy)

    def turn_comb():
        for copy in comb_cols:
            copy.wait_recv()
        for copy in comb_rows:
            go(copy)
        comb_in[pl.ds(x, 1)] = comb_mid[:, pl.ds(x, 1)].reshape(1, SIDE, *comb_in.shape[2:])

    def sem(c, half, i):
        return send.at[c, half, i], recv.at[c, half, i]

    def tile(half, c, j):
        u, v = uv[half]
        cols = pl.ds(*chunks[c])
        vj = mod4(v + j)
        if half == 0:
            rows = grad[pl.ds(vj, 1)]
        else:
            rows = grad[:, pl.ds(vj, 1)]
        out = contract(rows.reshape(group, 2 * ff), wgu[half, cols, :], 1, 1).astype(BF)
        up, down = at(half, u, mod4(v + 1)), at(half, u, mod4(v + 3))
        if j == 0:
            returned[pl.ds(half, 1), :, pl.ds(v, 1), :, cols] = out.reshape(1, SIDE, 1, SLOT, -1)
            return
        outgoing[half, j - 1, :, :, cols] = out.reshape(SIDE, SLOT, -1)
        piece = outgoing.at[half, j - 1]
        if j == 2:
            go(remote(piece.at[pl.ds(0, 2), :, cols], relayed.at[half, 0, :, :, cols], *sem(c, half, 0), expert=up))
            go(remote(piece.at[pl.ds(2, 2), :, cols], relayed.at[half, 1, :, :, cols], *sem(c, half, 1), expert=down))
        else:
            go(remote(
                piece.at[:, :, cols], returned.at[half, :, v, :, cols],
                *sem(c, half, 2 + j // 2), expert=up if j == 1 else down,
            ))

    def forward(half, c):
        u, v = uv[half]
        cols = pl.ds(*chunks[c])
        up, down = at(half, u, mod4(v + 1)), at(half, u, mod4(v + 3))
        for d, to, origin in ((0, up, mod4(v + 3)), (1, down, mod4(v + 1))):
            slot = relayed.at[half, d, :, :, cols]
            remote(slot, slot, *sem(c, half, d), expert=to).wait_recv()
            go(remote(slot, returned.at[half, pl.ds(2 * d, 2), origin, :, cols], *sem(c, half, 4 + d), expert=to))

    def turn(half, c):
        u, v = uv[half]
        start, size = chunks[c]
        cols = pl.ds(start, size)
        up, down = at(half, mod4(u + 1), v), at(half, mod4(u + 3), v)
        for d in (0, 1):
            piece = returned.at[half, :, 0, :, cols]
            remote(piece, piece, *sem(c, half, 2 + d), expert=up).wait_recv()
            piece = returned.at[half, pl.ds(0, 2), 0, :, cols]
            remote(piece, piece, *sem(c, half, 4 + d), expert=up).wait_recv()
        for o in (2, 1, 3, 0):
            uo = mod4(u + o)
            source = at(half, uo, v)
            maps = jnp.concatenate(
                [one_hot(table[pl.ds(source, 1), pl.ds(at(half, u, w), 1), :][0]) for w in range(SIDE)],
                axis=0,
            )
            rows = returned[pl.ds(half, 1), pl.ds(uo, 1), :, :, cols].reshape(group, size)
            total = contract(maps, rows, 0, 0)
            if o == 2:
                sending[half, 0, :, cols] = total.astype(BF)
                low, high = pl.ds(0, TOK // 2), pl.ds(TOK // 2, TOK // 2)
                go(remote(sending.at[half, 0, low, cols], half_in.at[half, 0, :, cols], *sem(c, half, 6), expert=up))
                go(remote(sending.at[half, 0, high, cols], half_in.at[half, 1, :, cols], *sem(c, half, 7), expert=down))
            else:
                partial[half, o // 2 if o else 2, :, pl.ds(0, size)] = total

    def add_up(half, c):
        u, v = uv[half]
        start, size = chunks[c]
        cols = pl.ds(start, size)
        up, down = at(half, mod4(u + 1), v), at(half, mod4(u + 3), v)
        for d, to in ((0, up), (1, down)):
            piece = half_in.at[half, d, :, cols]
            remote(piece, piece, *sem(c, half, 6 + d), expert=to).wait_recv()
            met = pl.ds(d * (TOK // 2), TOK // 2)
            other = pl.ds((1 - d) * (TOK // 2), TOK // 2)
            sending[half, 1 + d, met, cols] = (
                partial[half, d, met, pl.ds(0, size)] + half_in[half, d, :, cols].astype(F32)
            ).astype(BF)
            sending[half, 1 + d, other, cols] = partial[half, d, other, pl.ds(0, size)].astype(BF)
            go(remote(sending.at[half, 1 + d, :, cols], full_in.at[half, d, :, cols], *sem(c, half, 8 + d), expert=to))

    def finish(half, c):
        start, size = chunks[c]
        cols = pl.ds(start, size)
        for d in (0, 1):
            piece = full_in.at[half, d, :, cols]
            remote(piece, piece, *sem(c, half, 8 + d), expert=me).wait_recv()
        total = partial[half, 2, :, pl.ds(0, size)] + (
            full_in[half, 0, :, cols].astype(F32) + full_in[half, 1, :, cols].astype(F32)
        )
        place = pl.ds(half * width + start, size)
        final[:, place] = total.astype(BF)
        go(remote(final.at[:, place], passed.at[:, place], *sem(c, half, 10), pipe=mod4(pipe + 3)))

    busy = {}

    def put(key, copy):
        busy[key] = copy
        copy.start()

    def free(key):
        if key in busy:
            copy, away = busy.pop(key)
            copy.wait_send() if away else copy.wait()

    units = []
    gu_step = 256
    gu_count = width // gu_step
    dn_cuts = DN_CUTS

    def gate_up_unit(away, i):
        side = 1 - dp if away else dp
        n = (0 if away else gu_count) + i
        key = ("gu", n % 2)
        left = saved[pl.ds(side, 1), :, pl.ds(i * gu_step, gu_step)][0]
        out = contract(left, grad[...].reshape(SIDE * group, 2 * ff), 0, 0).astype(BF)
        free(key)
        gu_stage[n % 2] = out
        rows = pl.ds(i * gu_step, gu_step)
        if away:
            copy = remote(gu_stage.at[n % 2], gu_recv.at[rows], dw_send.at[i], dw_recv.at[i], dp=1 - dp)
            arrivals.append(copy)
        else:
            copy = pltpu.make_async_copy(gu_stage.at[n % 2], gu_own.at[rows], own_sem.at[i])
        copy.start()
        busy[key] = (copy, away)

    def down_unit(away, i):
        side = 1 - dp if away else dp
        n = (0 if away else len(dn_cuts)) + i
        key = ("dn", n % 2)
        rows = pl.ds(*dn_cuts[i])
        slot = dn_stage.at[n % 2, pl.ds(0, dn_cuts[i][1])]
        right = dy[pl.ds(side, 1)].reshape(SIDE * group, width)
        out = contract(scaled[:, rows], right, 0, 0).astype(BF)
        free(key)
        slot[...] = out
        if away:
            copy = remote(slot, dn_recv.at[rows], dw_send.at[gu_count + i], dw_recv.at[gu_count + i], dp=1 - dp)
            arrivals.append(copy)
        else:
            copy = pltpu.make_async_copy(slot, dn_own.at[rows], own_sem.at[gu_count + i])
        copy.start()
        busy[key] = (copy, away)

    arrivals = []
    for away in (True, False):
        units += [functools.partial(down_unit, away, i) for i in range(len(dn_cuts))]
        units += [functools.partial(gate_up_unit, away, i) for i in range(gu_count)]

    def work(count):
        for _ in range(min(count, len(units))):
            units.pop(0)()

    both = (0, 1)
    loads["wgu_own"].wait()
    loads["wgu_peer"].wait()
    for j in (2, 1, 3, 0):
        for half in both:
            tile(half, 0, j)
    for half in both:
        forward(half, 0)
    turn_comb()
    for j in (2, 1, 3, 0):
        for half in both:
            tile(half, 1, j)
    for name in ("scaled", "in0", "in1"):
        loads[name].wait()
    work(1)
    for half in both:
        forward(half, 1)
    work(2)
    for half in both:
        turn(half, 0)
    work(2)
    for half in both:
        add_up(half, 0)
    work(3)
    for half in both:
        finish(half, 0)
    work(3)
    for half in both:
        turn(half, 1)
    work(2)
    for half in both:
        add_up(half, 1)
    work(len(units))
    for half in both:
        finish(half, 1)
    for key in list(busy):
        free(key)
    for copy in arrivals + comb_rows:
        copy.wait_recv()
    for c, (start, size) in enumerate(chunks):
        for half in both:
            place = pl.ds(half * width + start, size)
            piece = passed.at[:, place]
            remote(piece, piece, *sem(c, half, 10), pipe=mod4(pipe + 3)).wait_recv()
    for copy in sends:
        copy.wait_send()


def backward(dya, dyb, table, wgu_own, wgu_peer, wdn_own, wdn_peer, coef, hidden, scaled, inputs):
    width = dya.shape[-1]
    rows, ff = hidden.shape
    group = SIDE * SLOT
    vmem = pl.BlockSpec(memory_space=pltpu.VMEM)
    anyw = pl.BlockSpec(memory_space=pltpu.HBM)
    widest = max(size for _, size in CHUNKS)
    cut = max(size for _, size in DN_CUTS)
    dma = pltpu.SemaphoreType.DMA
    return pl.pallas_call(
        backward_kernel,
        out_shape=(
            jax.ShapeDtypeStruct((TOK, 2 * width), BF),
            jax.ShapeDtypeStruct((SIDE, SIDE, 8, TOK), F32),
            jax.ShapeDtypeStruct(wgu_own.shape, BF),
            jax.ShapeDtypeStruct(wgu_own.shape, BF),
            jax.ShapeDtypeStruct(wdn_own.shape, BF),
            jax.ShapeDtypeStruct(wdn_own.shape, BF),
        ),
        in_specs=[anyw, anyw, vmem] + [anyw] * 8,
        out_specs=(anyw, vmem, anyw, anyw, anyw, anyw),
        scratch_shapes=[
            pltpu.VMEM((2,) + wgu_own.shape, BF),
            pltpu.VMEM((2,) + wdn_own.shape, BF),
            pltpu.VMEM((2, EXPERTS, SLOT, width), BF),
            pltpu.VMEM((2, rows, width), BF),
            pltpu.VMEM((rows, ff), BF),
            pltpu.VMEM((2, group, 2 * ff), F32),
            pltpu.VMEM((2, group, ff), F32),
            pltpu.VMEM((SIDE, SIDE, SLOT, 2 * ff), BF),
            pltpu.VMEM((2, 3, SIDE, SLOT, width), BF),
            pltpu.VMEM((2, SIDE, SIDE, SLOT, width), BF),
            pltpu.VMEM((2, 2, 2, SLOT, width), BF),
            pltpu.VMEM((2, 3, TOK, widest), F32),
            pltpu.VMEM((2, 3, TOK, width), BF),
            pltpu.VMEM((2, 2, TOK // 2, width), BF),
            pltpu.VMEM((2, 2, TOK, width), BF),
            pltpu.VMEM((TOK, 2 * width), BF),
            pltpu.VMEM((EXPERTS, 8, TOK), F32),
            pltpu.VMEM((SIDE, SIDE, 8, TOK), F32),
            pltpu.VMEM((2, 256, 2 * ff), BF),
            pltpu.VMEM((2, cut, width), BF),
            dma((9,)),
            dma((SIDE, 2)),
            dma((len(CHUNKS), 2, 11)),
            dma((len(CHUNKS), 2, 11)),
            dma((6,)),
            dma((6,)),
            dma((8,)),
            dma((8,)),
            dma((8,)),
        ],
        compiler_params=pltpu.CompilerParams(
            collective_id=1, has_side_effects=True, vmem_limit_bytes=64 * 1024 * 1024
        ),
        name="backward",
    )(dya, dyb, table, wgu_own, wgu_peer, wdn_own, wdn_peer, coef, hidden, scaled, inputs)


def body(out_grad, routes, combine, gate_up_weight, down_weight, saved_inputs, saved_gate_up):
    rt, cb = routes[0].T, combine[0].T.astype(F32)
    own_gu, own_dn = gate_up_weight[0, 0], down_weight[0, 0]
    dya, dyb, table, wgu_peer, wdn_peer, coef, hidden, scaled = dispatch(
        out_grad[0], rt, cb, own_gu, own_dn, saved_gate_up[0, 0, 0]
    )
    passed, comb, gu_own, gu_recv, dn_own, dn_recv = backward(
        dya, dyb, table, own_gu, wgu_peer, own_dn, wdn_peer, coef, hidden, scaled, saved_inputs[0, 0, 0]
    )
    by_expert = jnp.swapaxes(comb[:, :, 0, :], 0, 1).reshape(EXPERTS, TOK)
    ids = jnp.arange(EXPERTS, dtype=jnp.int32)
    comb_grad = jnp.sum(jnp.where(rt[:, None, :] == ids[None, :, None], by_expert[None], 0.0), axis=1)
    sum_gu = (gu_own.astype(F32) + gu_recv.astype(F32)).astype(BF)
    sum_dn = (dn_own.astype(F32) + dn_recv.astype(F32)).astype(BF)
    return passed[None], comb_grad.T.astype(BF)[None], sum_gu[None, None], sum_dn[None, None]


def solution(mesh):
    placed = (
        P("pipe", ("dp", "expert"), None),
        P("pipe", ("dp", "expert"), None),
        P("pipe", ("dp", "expert"), None),
        P("pipe", "expert", "dp", None),
        P("pipe", "expert", None, "dp"),
        P("pipe", "dp", "expert", None, None),
        P("pipe", "dp", "expert", None, None),
    )
    return jax.shard_map(
        body,
        mesh=mesh,
        in_specs=placed,
        out_specs=(
            P("pipe", ("dp", "expert"), None),
            P("pipe", ("dp", "expert"), None),
            P("pipe", "expert", "dp", None),
            P("pipe", "expert", None, "dp"),
        ),
        check_vma=False,
    )
```

```python
import functools

import jax
import jax.numpy as jnp
from jax import lax
from jax.experimental import pallas as pl
from jax.experimental.pallas import tpu as pltpu
from jax.sharding import PartitionSpec as P

SLOT = 64
SIDE = 4
TOK = 128
EXPERTS = 16
TOP = 6
MESH = pl.DeviceIdType.MESH
BF = jnp.bfloat16
F32 = jnp.float32
ORDER = (0, 1, 3, 2)
PLACE = (0, 1, 3, 2)
CHUNKS = ((0, 768), (768, 512))
GU_STEP = 256
DN_CUTS = ((0, 256), (256, 256), (512, 384))
BOTH = (0, 1)
PACE = (5, 2, 2, 3, 2, 2)
LOW, HIGH = pl.ds(0, TOK // 2), pl.ds(TOK // 2, TOK // 2)


def mod4(i):
    return lax.rem(i, SIDE)


def at(half, u, v):
    return v * SIDE + u if half == 0 else u * SIDE + v


def remote(src, dst, send, recv, **where):
    return pltpu.make_async_remote_copy(
        src_ref=src, dst_ref=dst, send_sem=send, recv_sem=recv, device_id=where, device_id_type=MESH
    )


def enter(**peers):
    barrier = pltpu.get_barrier_semaphore()
    count = 0
    for axis, indices in peers.items():
        for index in indices:
            pl.semaphore_signal(barrier, inc=1, device_id={axis: index}, device_id_type=MESH)
            count += 1
    pl.semaphore_wait(barrier, count)


def same_slot(slots_row):
    ids = lax.broadcasted_iota(jnp.int32, (SLOT, TOK), 0).astype(F32)
    return ids == slots_row


def one_hot(slots_row):
    return jnp.where(same_slot(slots_row), 1.0, 0.0).astype(BF)


def contract(a, b, da, db):
    return lax.dot_general(a, b, (((da,), (db,)), ((), ())), preferred_element_type=F32)


def layer_kernel(
    tok, picks, wgu_in, wdn_in, inputs_in, gate_up_in,
    passed, comb_grad, gu_grad, dn_grad, gu_part, dn_part,
    wgu, wdn, dy, saved, grad, scaled, table,
    gathered, staged, outgoing, returned, partial, sending, half_in, full_in, final,
    comb_out, comb_mid, comb_in, gu_stage, dn_stage, gu_other, dn_other,
    load_sem, held_sem, saved_sem, ring_send, ring_recv, slot_send, slot_recv, table_send, table_recv,
    dp_send, dp_recv, back_send, back_recv, comb_send, comb_recv, dw_send, dw_recv, own_sem, other_sem,
):
    me = lax.axis_index("expert")
    dp = lax.axis_index("dp")
    pipe = lax.axis_index("pipe")
    y, x = lax.div(me, SIDE), lax.rem(me, SIDE)
    width = dy.shape[-1]
    ff = scaled.shape[-1]
    group = SIDE * SLOT
    uv = ((x, y), (y, x))
    row_peers = [y * SIDE + mod4(x + i) for i in (1, 2, 3)]
    col_peers = [mod4(y + i) * SIDE + x for i in (1, 2, 3)]

    loads = {}

    def load(name, src, dst, sem):
        loads[name] = pltpu.make_async_copy(src, dst, sem)
        loads[name].start()

    def need(*names):
        for name in names:
            if name in loads:
                loads.pop(name).wait()

    def block_rows(i, k):
        source = mod4(y + ORDER[i]) * SIDE + mod4(x + ORDER[k])
        return source, pl.ds(pl.multiple_of(source * SLOT, SLOT), SLOT)

    enter(
        expert=row_peers + col_peers,
        dp=[1 - dp],
        pipe=[mod4(pipe + 1), mod4(pipe + 3)],
    )
    sends = []

    def go(copy):
        copy.start()
        sends.append(copy)
        return copy

    def ring(half, step):
        u, v = uv[half]
        up, down = at(half, mod4(u + 1), v), at(half, mod4(u + 3), v)
        if step == 0:
            mine = tok.at[:, pl.ds(half * width, width)]
            return (
                remote(mine, gathered.at[half, 0], ring_send.at[half, 0], ring_recv.at[half, 0], expert=down),
                remote(mine, gathered.at[half, 1], ring_send.at[half, 1], ring_recv.at[half, 1], expert=up),
            )
        return (
            remote(
                gathered.at[half, 0, LOW], gathered.at[half, 2, LOW],
                ring_send.at[half, 2], ring_recv.at[half, 2], expert=down,
            ),
            remote(
                gathered.at[half, 1, HIGH], gathered.at[half, 2, HIGH],
                ring_send.at[half, 3], ring_recv.at[half, 3], expert=up,
            ),
        )

    near = [ring(half, 0) for half in BOTH]
    for half in BOTH:
        for copy in near[half]:
            go(copy)

    ids = lax.broadcasted_iota(jnp.int32, (EXPERTS, TOK), 0).astype(F32)
    chosen = jnp.zeros((EXPERTS, TOK), F32)
    weight = jnp.zeros((EXPERTS, TOK), F32)
    for k in range(TOP):
        hit = jnp.where(ids == picks[pl.ds(k, 1), :], 1.0, 0.0)
        chosen = chosen + hit
        weight = weight + hit * picks[pl.ds(TOP + k, 1), :]
    before = lax.broadcasted_iota(jnp.int32, (TOK, TOK), 0) < lax.broadcasted_iota(
        jnp.int32, (TOK, TOK), 1
    )
    count = jnp.dot(
        chosen.astype(BF), jnp.where(before, 1.0, 0.0).astype(BF), preferred_element_type=F32
    )
    slots = jnp.where(chosen > 0.5, count, -1.0)
    table[pl.ds(me, 1)] = jnp.concatenate([slots, weight], axis=0)[None]

    row_tables = [
        remote(table.at[me], table.at[me], table_send.at[i], table_recv.at[i], expert=row_peers[i])
        for i in range(3)
    ]
    for copy in row_tables:
        go(copy)
    across = [
        remote(wdn_in, wdn.at[dp], dp_send.at[0], dp_recv.at[0], dp=1 - dp),
        remote(wgu_in, wgu.at[dp], dp_send.at[1], dp_recv.at[1], dp=1 - dp),
    ]
    for copy in across:
        go(copy)
    load("wdn", wdn_in, wdn.at[dp], load_sem.at[0])
    for i in range(SIDE):
        for k in range(SIDE):
            load(("held", i, k), gate_up_in.at[block_rows(i, k)[1]], grad.at[i, k], held_sem.at[i, k])
    load("wgu", wgu_in, wgu.at[dp], load_sem.at[1])
    for i in range(SIDE):
        for k in range(SIDE):
            load(("saved", i, k), inputs_in.at[block_rows(i, k)[1]], saved.at[i, k], saved_sem.at[i, k])

    def slots_of(source, expert):
        return table[pl.ds(source, 1), pl.ds(expert, 1), :][0]

    arrivals = {}

    def arrived(half, r, j):
        if (half, r, j) in arrivals:
            arrivals.pop((half, r, j)).wait_recv()

    def deliver(half, r):
        u, v = uv[half]
        source = at(half, mod4(u + ORDER[r]), v)
        maps = [one_hot(slots_of(source, at(half, u, mod4(v + j)))) for j in (2, 1, 3, 0)]
        if r == 0:
            block = tok[:, pl.ds(half * width, width)]
        else:
            block = gathered[half, r - 1]
        rows = jnp.dot(jnp.concatenate(maps, axis=0), block, preferred_element_type=F32)
        rows = rows.astype(BF).reshape(SIDE, SLOT, width)
        for n, j in enumerate((2, 1, 3, 0)):
            there = PLACE[(SIDE - j) % SIDE]
            i, k = (there, r) if half == 0 else (r, there)
            if j == 0:
                dy[half, i, k] = rows[n]
            else:
                staged[half, j - 1, r] = rows[n]
                copy = remote(
                    staged.at[half, j - 1, r], dy.at[half, i, k],
                    slot_send.at[half, r, j - 1], slot_recv.at[half, r, j - 1],
                    expert=at(half, u, mod4(v + j)),
                )
                go(copy)
                arrivals[(half, r, j)] = copy

    def through_rows(blocks):
        need("wdn", "wdn_peer", *[("held", i, k) for i, k in blocks])
        for i, k in blocks:
            arrived(0, k, (SIDE - ORDER[i]) % SIDE)
            arrived(1, i, (SIDE - ORDER[k]) % SIDE)
        through = contract(jnp.concatenate([dy[0, i, k] for i, k in blocks], axis=0), wdn[0], 1, 1)
        through = through + contract(
            jnp.concatenate([dy[1, i, k] for i, k in blocks], axis=0), wdn[1], 1, 1
        )
        for n, (i, k) in enumerate(blocks):
            source = block_rows(i, k)[0]
            part = through[n * SLOT : (n + 1) * SLOT]
            same = same_slot(slots_of(source, me))
            given = table[pl.ds(source, 1), pl.ds(EXPERTS + me, 1), :][0]
            factor = jnp.sum(jnp.where(same, given, 0.0), axis=1, keepdims=True)
            gate = grad[i, k, :, pl.ds(0, ff)].astype(F32)
            up = grad[i, k, :, pl.ds(ff, ff)].astype(F32)
            logistic = 1.0 / (1.0 + jnp.exp(-gate))
            active = gate * logistic
            hidden = active * up
            comb = jnp.sum(part * hidden, axis=1, keepdims=True).astype(BF).astype(F32)
            row = jnp.sum(jnp.where(same, comb, 0.0), axis=0, keepdims=True)
            comb_out[i, k] = jnp.broadcast_to(row, comb_out.shape[2:])
            scaled[i, k] = (factor * hidden).astype(BF)
            weighted = factor * part
            slope = up * logistic * (1.0 + gate * (1.0 - logistic))
            grad[i, k, :, pl.ds(0, ff)] = (weighted * slope).astype(BF)
            grad[i, k, :, pl.ds(ff, ff)] = (weighted * active).astype(BF)

    def sem(c, half, i):
        return back_send.at[c, half, i], back_recv.at[c, half, i]

    waits = {}

    def tiles(half, c, pieces):
        u, v = uv[half]
        cols = pl.ds(*CHUNKS[c])
        rows = []
        for j, first, last, _ in pieces:
            for k in range(first, last):
                rows.append(grad[PLACE[j], k] if half == 0 else grad[k, PLACE[j]])
        out = contract(jnp.concatenate(rows, axis=0), wgu[half, cols, :], 1, 1).astype(BF)
        n = 0
        for j, first, last, number in pieces:
            span = last - first
            part = out[n * SLOT : (n + span) * SLOT].reshape(span, SLOT, -1)
            n += span
            if j == 0:
                returned[half, pl.ds(first, span), 0, :, cols] = part
                continue
            outgoing[half, j - 1, pl.ds(first, span), :, cols] = part
            copy = remote(
                outgoing.at[half, j - 1, pl.ds(first, span), :, cols],
                returned.at[half, pl.ds(first, span), PLACE[SIDE - j], :, cols],
                *sem(c, half, number),
                expert=at(half, u, mod4(v + j)),
            )
            go(copy)
            waits.setdefault((half, c), []).append(copy)

    def turn(half, c):
        u, v = uv[half]
        start, size = CHUNKS[c]
        cols = pl.ds(start, size)
        up, down = at(half, mod4(u + 1), v), at(half, mod4(u + 3), v)
        for copy in waits[(half, c)]:
            copy.wait_recv()
        for o in (2, 1, 3, 0):
            source = at(half, mod4(u + o), v)
            maps = jnp.concatenate(
                [one_hot(slots_of(source, at(half, u, mod4(v + w)))) for w in ORDER], axis=0
            )
            total = contract(maps, returned[half, PLACE[o], :, :, cols].reshape(group, size), 0, 0)
            if o == 2:
                sending[half, 0, :, cols] = total.astype(BF)
                go(remote(sending.at[half, 0, LOW, cols], half_in.at[half, 0, :, cols], *sem(c, half, 5), expert=up))
                go(remote(sending.at[half, 0, HIGH, cols], half_in.at[half, 1, :, cols], *sem(c, half, 6), expert=down))
            else:
                partial[half, (2, 0, 2, 1)[o], :, pl.ds(0, size)] = total

    def add_up(half, c):
        u, v = uv[half]
        start, size = CHUNKS[c]
        cols = pl.ds(start, size)
        up, down = at(half, mod4(u + 1), v), at(half, mod4(u + 3), v)
        for d, to, met, other in ((0, up, LOW, HIGH), (1, down, HIGH, LOW)):
            piece = half_in.at[half, d, :, cols]
            remote(piece, piece, *sem(c, half, 5 + d), expert=to).wait_recv()
            sending[half, 1 + d, met, cols] = (
                partial[half, d, met, pl.ds(0, size)] + half_in[half, d, :, cols].astype(F32)
            ).astype(BF)
            sending[half, 1 + d, other, cols] = partial[half, d, other, pl.ds(0, size)].astype(BF)
            go(remote(sending.at[half, 1 + d, :, cols], full_in.at[half, d, :, cols], *sem(c, half, 7 + d), expert=to))

    def finish(half, c):
        u, v = uv[half]
        start, size = CHUNKS[c]
        cols = pl.ds(start, size)
        for d, to in ((0, at(half, mod4(u + 1), v)), (1, at(half, mod4(u + 3), v))):
            piece = full_in.at[half, d, :, cols]
            remote(piece, piece, *sem(c, half, 7 + d), expert=to).wait_recv()
        total = partial[half, 2, :, pl.ds(0, size)] + (
            full_in[half, 0, :, cols].astype(F32) + full_in[half, 1, :, cols].astype(F32)
        )
        place = pl.ds(half * width + start, size)
        final[:, place] = total.astype(BF)
        go(remote(final.at[:, place], passed.at[:, place], *sem(c, half, 9), pipe=mod4(pipe + 3)))

    gu_count = width // GU_STEP
    busy = {}
    others = {}

    def free(key):
        if key in busy:
            copy, away = busy.pop(key)
            copy.wait_send() if away else copy.wait()

    def fetch(kind, i):
        n = i if kind == "gu" else gu_count + i
        ref, other = (gu_part, gu_other) if kind == "gu" else (dn_part, dn_other)
        rows = pl.ds(i * GU_STEP, GU_STEP) if kind == "gu" else pl.ds(*DN_CUTS[i])
        piece = ref.at[rows]
        remote(piece, piece, dw_send.at[n], dw_recv.at[n], dp=1 - dp).wait_recv()
        copy = pltpu.make_async_copy(piece, other.at[pl.ds(0, rows.size)], other_sem.at[n])
        copy.start()
        others[(kind, i)] = copy

    def grad_unit(kind, away, i):
        side = 1 - dp if away else dp
        if kind == "gu":
            count, n, rows = gu_count, i, pl.ds(i * GU_STEP, GU_STEP)
            cols = pl.ds(pl.multiple_of(side * width + i * GU_STEP, GU_STEP), GU_STEP)
            left = saved[:, :, :, cols].reshape(SIDE * group, GU_STEP)
            right = grad[...].reshape(SIDE * group, 2 * ff)
            stage, part, own, other = gu_stage, gu_part, gu_grad, gu_other
        else:
            count, n, rows = len(DN_CUTS), gu_count + i, pl.ds(*DN_CUTS[i])
            left = scaled[:, :, :, rows].reshape(SIDE * group, rows.size)
            right = dy[pl.ds(side, 1)].reshape(SIDE * group, width)
            stage, part, own, other = dn_stage, dn_part, dn_grad, dn_other
        turn_no = (0 if away else count) + i
        key = (kind, turn_no % 2)
        out = contract(left, right, 0, 0)
        free(key)
        slot = stage.at[turn_no % 2, pl.ds(0, rows.size)]
        if away:
            slot[...] = out.astype(BF)
            copy = remote(slot, part.at[rows], dw_send.at[n], dw_recv.at[n], dp=1 - dp)
        else:
            others.pop((kind, i)).wait()
            slot[...] = (out + other[pl.ds(0, rows.size), :].astype(F32)).astype(BF)
            if i + 1 < count:
                fetch(kind, i + 1)
            copy = pltpu.make_async_copy(slot, own.at[rows], own_sem.at[n])
        copy.start()
        busy[key] = (copy, away)

    units = [functools.partial(grad_unit, "dn", True, i) for i in range(len(DN_CUTS))]
    units += [functools.partial(grad_unit, "gu", True, i) for i in range(gu_count)]
    units += [functools.partial(fetch, "dn", 0), functools.partial(fetch, "gu", 0)]
    units += [functools.partial(grad_unit, "dn", False, i) for i in range(len(DN_CUTS))]
    units += [functools.partial(grad_unit, "gu", False, i) for i in range(gu_count)]

    def work(count):
        for _ in range(min(count, len(units))):
            units.pop(0)()

    for half in BOTH:
        deliver(half, 0)
    for copy in row_tables:
        copy.wait_recv()
    mine = pl.ds(y * SIDE, SIDE)
    col_tables = [
        remote(table.at[mine], table.at[mine], table_send.at[3 + i], table_recv.at[3 + i], expert=col_peers[i])
        for i in range(3)
    ]
    for copy in col_tables:
        go(copy)
    for half in BOTH:
        for copy in near[half]:
            copy.wait_recv()
        for copy in ring(half, 1):
            go(copy)
    for copy in col_tables:
        copy.wait_recv()
    for r in (1, 2):
        for half in BOTH:
            deliver(half, r)
    for half in BOTH:
        for copy in ring(half, 1):
            copy.wait_recv()
        deliver(half, 3)
    across[0].wait_recv()
    through_rows([(0, 0)])
    through_rows([(0, 1), (1, 0), (1, 1)])
    through_rows([(0, 2), (2, 0), (1, 2), (2, 1), (2, 2)])
    across[1].wait_recv()
    need("wgu")
    for c in BOTH:
        for half in BOTH:
            tiles(half, c, ((1, 0, 3, 0), (3, 0, 3, 1), (0, 0, 3, None)))
    through_rows([(0, 3), (3, 0), (1, 3), (3, 1)])
    through_rows([(2, 3), (3, 2), (3, 3)])
    comb_cols = [
        remote(
            comb_out.at[PLACE[i]], comb_mid.at[PLACE[SIDE - i]],
            comb_send.at[i - 1], comb_recv.at[i - 1], expert=col_peers[i - 1],
        )
        for i in (1, 2, 3)
    ]
    comb_rows = [
        remote(
            comb_mid.at[:, PLACE[i]], comb_in.at[PLACE[SIDE - i]],
            comb_send.at[2 + i], comb_recv.at[2 + i], expert=row_peers[i - 1],
        )
        for i in (1, 2, 3)
    ]
    comb_mid[0] = comb_out[0]
    for copy in comb_cols:
        go(copy)
    for c in BOTH:
        for half in BOTH:
            tiles(half, c, ((2, 0, 4, 2), (1, 3, 4, 3), (3, 3, 4, 4), (0, 3, 4, None)))
    for copy in comb_cols:
        copy.wait_recv()
    for copy in comb_rows:
        go(copy)
    comb_in[0] = comb_mid[:, 0]
    need(*[("saved", i, k) for i in range(SIDE) for k in range(SIDE)])
    work(PACE[0])
    for half in BOTH:
        turn(half, 0)
    work(PACE[1])
    for half in BOTH:
        add_up(half, 0)
    work(PACE[2])
    for half in BOTH:
        finish(half, 0)
    work(PACE[3])
    for half in BOTH:
        turn(half, 1)
    work(PACE[4])
    for half in BOTH:
        add_up(half, 1)
    work(PACE[5])
    for half in BOTH:
        finish(half, 1)
    work(len(units))
    for copy in comb_rows:
        copy.wait_recv()
    for k in range(TOP):
        total = jnp.zeros((1, TOK), F32)
        for i in range(SIDE):
            for j in range(SIDE):
                expert = mod4(y + ORDER[i]) * SIDE + mod4(x + ORDER[j])
                hit = picks[pl.ds(k, 1), :] == expert.astype(F32)
                total = total + jnp.where(hit, comb_in[j, i, pl.ds(0, 1), :], 0.0)
        comb_grad[pl.ds(k, 1), :] = total
    for key in list(busy):
        free(key)
    for c, (start, size) in enumerate(CHUNKS):
        for half in BOTH:
            place = pl.ds(half * width + start, size)
            piece = passed.at[:, place]
            remote(piece, piece, *sem(c, half, 9), pipe=mod4(pipe + 3)).wait_recv()
    for copy in sends:
        copy.wait_send()


def layer(tok, picks, wgu, wdn, inputs, gate_up):
    width, both = wgu.shape
    ff = both // 2
    vmem = pl.BlockSpec(memory_space=pltpu.VMEM)
    hbm = pl.BlockSpec(memory_space=pltpu.HBM)
    widest = max(size for _, size in CHUNKS)
    cut = max(size for _, size in DN_CUTS)
    count = width // GU_STEP + len(DN_CUTS)
    dma = pltpu.SemaphoreType.DMA
    return pl.pallas_call(
        layer_kernel,
        out_shape=(
            jax.ShapeDtypeStruct((TOK, 2 * width), BF),
            jax.ShapeDtypeStruct((TOP, TOK), F32),
            jax.ShapeDtypeStruct(wgu.shape, BF),
            jax.ShapeDtypeStruct(wdn.shape, BF),
            jax.ShapeDtypeStruct(wgu.shape, BF),
            jax.ShapeDtypeStruct(wdn.shape, BF),
        ),
        in_specs=[vmem, vmem, hbm, hbm, hbm, hbm],
        out_specs=(hbm, vmem, hbm, hbm, hbm, hbm),
        scratch_shapes=[
            pltpu.VMEM((2,) + wgu.shape, BF),
            pltpu.VMEM((2,) + wdn.shape, BF),
            pltpu.VMEM((2, SIDE, SIDE, SLOT, width), BF),
            pltpu.VMEM((SIDE, SIDE, SLOT, 2 * width), BF),
            pltpu.VMEM((SIDE, SIDE, SLOT, both), BF),
            pltpu.VMEM((SIDE, SIDE, SLOT, ff), BF),
            pltpu.VMEM((EXPERTS, 2 * EXPERTS, TOK), F32),
            pltpu.VMEM((2, 3, TOK, width), BF),
            pltpu.VMEM((2, 3, SIDE, SLOT, width), BF),
            pltpu.VMEM((2, 3, SIDE, SLOT, width), BF),
            pltpu.VMEM((2, SIDE, SIDE, SLOT, width), BF),
            pltpu.VMEM((2, 3, TOK, widest), F32),
            pltpu.VMEM((2, 3, TOK, width), BF),
            pltpu.VMEM((2, 2, TOK // 2, width), BF),
            pltpu.VMEM((2, 2, TOK, width), BF),
            pltpu.VMEM((TOK, 2 * width), BF),
            pltpu.VMEM((SIDE, SIDE, 8, TOK), F32),
            pltpu.VMEM((SIDE, SIDE, 8, TOK), F32),
            pltpu.VMEM((SIDE, SIDE, 8, TOK), F32),
            pltpu.VMEM((2, GU_STEP, both), BF),
            pltpu.VMEM((2, cut, width), BF),
            pltpu.VMEM((GU_STEP, both), BF),
            pltpu.VMEM((cut, width), BF),
            dma((2,)),
            dma((SIDE, SIDE)),
            dma((SIDE, SIDE)),
            dma((2, 4)),
            dma((2, 4)),
            dma((2, SIDE, 3)),
            dma((2, SIDE, 3)),
            dma((6,)),
            dma((6,)),
            dma((2,)),
            dma((2,)),
            dma((len(CHUNKS), 2, 10)),
            dma((len(CHUNKS), 2, 10)),
            dma((6,)),
            dma((6,)),
            dma((count,)),
            dma((count,)),
            dma((count,)),
            dma((count,)),
        ],
        compiler_params=pltpu.CompilerParams(
            collective_id=0, has_side_effects=True, vmem_limit_bytes=64 * 1024 * 1024
        ),
        name="layer",
    )(tok, picks, wgu, wdn, inputs, gate_up)


def body(out_grad, routes, combine, gate_up_weight, down_weight, saved_inputs, saved_gate_up):
    picks = jnp.concatenate([routes[0].T.astype(F32), combine[0].T.astype(F32)], axis=0)
    passed, comb, gu_grad, dn_grad, _, _ = layer(
        out_grad[0], picks, gate_up_weight[0, 0], down_weight[0, 0], saved_inputs[0, 0, 0], saved_gate_up[0, 0, 0]
    )
    return passed[None], comb.T.astype(BF)[None], gu_grad[None, None], dn_grad[None, None]


def solution(mesh):
    placed = (
        P("pipe", ("dp", "expert"), None),
        P("pipe", ("dp", "expert"), None),
        P("pipe", ("dp", "expert"), None),
        P("pipe", "expert", "dp", None),
        P("pipe", "expert", None, "dp"),
        P("pipe", "dp", "expert", None, None),
        P("pipe", "dp", "expert", None, None),
    )
    return jax.shard_map(
        body,
        mesh=mesh,
        in_specs=placed,
        out_specs=(
            P("pipe", ("dp", "expert"), None),
            P("pipe", ("dp", "expert"), None),
            P("pipe", "expert", "dp", None),
            P("pipe", "expert", None, "dp"),
        ),
        check_vma=False,
    )
```

```python
import functools

import jax
import jax.numpy as jnp
from jax import lax
from jax.experimental import pallas as pl
from jax.experimental.pallas import tpu as pltpu
from jax.sharding import PartitionSpec as P

SLOT = 64
SIDE = 4
TOK = 128
EXPERTS = 16
TOP = 6
MESH = pl.DeviceIdType.MESH
BF = jnp.bfloat16
F32 = jnp.float32
ORDER = (0, 1, 3, 2)
PLACE = (0, 1, 3, 2)
CHUNKS = ((0, 512), (512, 512), (1024, 256))
GU_STEP = 256
DN_CUTS = ((0, 256), (256, 256), (512, 384))
BOTH = (0, 1)
STEPS = (
    (7, "turn", 0), (1, "add", 0), (2, "turn", 1), (1, "finish", 0), (1, "add", 1),
    (2, "turn", 2), (1, "finish", 1), (1, "add", 2), (1, "finish", 2),
)
KEEP = (2, 10, 7)
LOW, HIGH = pl.ds(0, TOK // 2), pl.ds(TOK // 2, TOK // 2)


def mod4(i):
    return lax.rem(i, SIDE)


def at(half, u, v):
    return v * SIDE + u if half == 0 else u * SIDE + v


def remote(src, dst, send, recv, **where):
    return pltpu.make_async_remote_copy(
        src_ref=src, dst_ref=dst, send_sem=send, recv_sem=recv, device_id=where, device_id_type=MESH
    )


def greet(barrier, **peers):
    count = 0
    for axis, indices in peers.items():
        for index in indices:
            pl.semaphore_signal(barrier, inc=1, device_id={axis: index}, device_id_type=MESH)
            count += 1
    return count


def same_slot(slots_row):
    ids = lax.broadcasted_iota(jnp.int32, (SLOT, TOK), 0).astype(F32)
    return ids == slots_row


def one_hot(slots_row):
    return jnp.where(same_slot(slots_row), 1.0, 0.0).astype(BF)


def contract(a, b, da, db):
    return lax.dot_general(a, b, (((da,), (db,)), ((), ())), preferred_element_type=F32)


def layer_kernel(
    tok, picks, wgu_in, wdn_in, inputs_in, gate_up_in,
    passed, comb_grad, gu_grad, dn_grad, gu_part, dn_part,
    wgu, wdn, dy, saved, grad, scaled, table,
    gathered, staged, outgoing, returned, partial, sending, half_in, full_in, final,
    comb_out, comb_mid, comb_in, gu_stage, dn_stage, gu_other, dn_other,
    load_sem, held_sem, saved_sem, ring_send, ring_recv, slot_send, slot_recv, table_send, table_recv,
    dp_send, dp_recv, back_send, back_recv, comb_send, comb_recv, dw_send, dw_recv, own_sem, other_sem,
):
    me = lax.axis_index("expert")
    dp = lax.axis_index("dp")
    pipe = lax.axis_index("pipe")
    y, x = lax.div(me, SIDE), lax.rem(me, SIDE)
    width = dy.shape[-1]
    ff = scaled.shape[-1]
    group = SIDE * SLOT
    uv = ((x, y), (y, x))
    row_peers = [y * SIDE + mod4(x + i) for i in (1, 2, 3)]
    col_peers = [mod4(y + i) * SIDE + x for i in (1, 2, 3)]

    loads = {}

    def load(name, src, dst, sem):
        loads[name] = pltpu.make_async_copy(src, dst, sem)
        loads[name].start()

    def need(*names):
        for name in names:
            if name in loads:
                loads.pop(name).wait()

    def block_rows(i, k):
        source = mod4(y + ORDER[i]) * SIDE + mod4(x + ORDER[k])
        return source, pl.ds(pl.multiple_of(source * SLOT, SLOT), SLOT)

    barrier = pltpu.get_barrier_semaphore()
    greeted = greet(
        barrier,
        expert=row_peers + col_peers,
        dp=[1 - dp],
        pipe=[mod4(pipe + 1), mod4(pipe + 3)],
    )
    sends = []

    def go(copy):
        copy.start()
        sends.append(copy)
        return copy

    def ring(half, step):
        u, v = uv[half]
        up, down = at(half, mod4(u + 1), v), at(half, mod4(u + 3), v)
        if step == 0:
            mine = tok.at[:, pl.ds(half * width, width)]
            return (
                remote(mine, gathered.at[half, 0], ring_send.at[half, 0], ring_recv.at[half, 0], expert=down),
                remote(mine, gathered.at[half, 1], ring_send.at[half, 1], ring_recv.at[half, 1], expert=up),
            )
        return (
            remote(
                gathered.at[half, 0, LOW], gathered.at[half, 2, LOW],
                ring_send.at[half, 2], ring_recv.at[half, 2], expert=down,
            ),
            remote(
                gathered.at[half, 1, HIGH], gathered.at[half, 2, HIGH],
                ring_send.at[half, 3], ring_recv.at[half, 3], expert=up,
            ),
        )

    load("wdn", wdn_in, wdn.at[dp], load_sem.at[0])
    for i in range(SIDE):
        for k in range(SIDE):
            load(("held", i, k), gate_up_in.at[block_rows(i, k)[1]], grad.at[i, k], held_sem.at[i, k])
    load("wgu", wgu_in, wgu.at[dp], load_sem.at[1])
    for i in range(SIDE):
        for k in range(SIDE):
            load(("saved", i, k), inputs_in.at[block_rows(i, k)[1]], saved.at[i, k], saved_sem.at[i, k])

    ids = lax.broadcasted_iota(jnp.int32, (EXPERTS, TOK), 0).astype(F32)
    chosen = jnp.zeros((EXPERTS, TOK), F32)
    weight = jnp.zeros((EXPERTS, TOK), F32)
    for k in range(TOP):
        hit = jnp.where(ids == picks[pl.ds(k, 1), :], 1.0, 0.0)
        chosen = chosen + hit
        weight = weight + hit * picks[pl.ds(TOP + k, 1), :]
    before = lax.broadcasted_iota(jnp.int32, (TOK, TOK), 0) < lax.broadcasted_iota(
        jnp.int32, (TOK, TOK), 1
    )
    count = jnp.dot(
        chosen.astype(BF), jnp.where(before, 1.0, 0.0).astype(BF), preferred_element_type=F32
    )
    slots = jnp.where(chosen > 0.5, count, -1.0)
    table[pl.ds(me, 1)] = jnp.concatenate([slots, weight], axis=0)[None]

    pl.semaphore_wait(barrier, greeted)
    near = [ring(half, 0) for half in BOTH]
    for half in BOTH:
        for copy in near[half]:
            go(copy)

    row_tables = [
        remote(table.at[me], table.at[me], table_send.at[i], table_recv.at[i], expert=row_peers[i])
        for i in range(3)
    ]
    for copy in row_tables:
        go(copy)
    across = [
        remote(wdn_in, wdn.at[dp], dp_send.at[0], dp_recv.at[0], dp=1 - dp),
        remote(wgu_in, wgu.at[dp], dp_send.at[1], dp_recv.at[1], dp=1 - dp),
    ]
    for copy in across:
        go(copy)
    def slots_of(source, expert):
        return table[pl.ds(source, 1), pl.ds(expert, 1), :][0]

    arrivals = {}

    def arrived(half, r, j):
        if (half, r, j) in arrivals:
            arrivals.pop((half, r, j)).wait_recv()

    def deliver(half, r):
        u, v = uv[half]
        source = at(half, mod4(u + ORDER[r]), v)
        maps = [one_hot(slots_of(source, at(half, u, mod4(v + j)))) for j in (2, 1, 3, 0)]
        if r == 0:
            block = tok[:, pl.ds(half * width, width)]
        else:
            block = gathered[half, r - 1]
        rows = jnp.dot(jnp.concatenate(maps, axis=0), block, preferred_element_type=F32)
        rows = rows.astype(BF).reshape(SIDE, SLOT, width)
        for n, j in enumerate((2, 1, 3, 0)):
            there = PLACE[(SIDE - j) % SIDE]
            i, k = (there, r) if half == 0 else (r, there)
            if j == 0:
                dy[half, i, k] = rows[n]
            else:
                staged[half, j - 1, r] = rows[n]
                copy = remote(
                    staged.at[half, j - 1, r], dy.at[half, i, k],
                    slot_send.at[half, r, j - 1], slot_recv.at[half, r, j - 1],
                    expert=at(half, u, mod4(v + j)),
                )
                go(copy)
                arrivals[(half, r, j)] = copy

    def through_rows(blocks):
        need("wdn", "wdn_peer", *[("held", i, k) for i, k in blocks])
        for i, k in blocks:
            arrived(0, k, (SIDE - ORDER[i]) % SIDE)
            arrived(1, i, (SIDE - ORDER[k]) % SIDE)
        through = contract(jnp.concatenate([dy[0, i, k] for i, k in blocks], axis=0), wdn[0], 1, 1)
        through = through + contract(
            jnp.concatenate([dy[1, i, k] for i, k in blocks], axis=0), wdn[1], 1, 1
        )
        for n, (i, k) in enumerate(blocks):
            source = block_rows(i, k)[0]
            part = through[n * SLOT : (n + 1) * SLOT]
            same = same_slot(slots_of(source, me))
            given = table[pl.ds(source, 1), pl.ds(EXPERTS + me, 1), :][0]
            factor = jnp.sum(jnp.where(same, given, 0.0), axis=1, keepdims=True)
            gate = grad[i, k, :, pl.ds(0, ff)].astype(F32)
            up = grad[i, k, :, pl.ds(ff, ff)].astype(F32)
            logistic = 1.0 / (1.0 + jnp.exp(-gate))
            active = gate * logistic
            hidden = active * up
            comb = jnp.sum(part * hidden, axis=1, keepdims=True).astype(BF).astype(F32)
            row = jnp.sum(jnp.where(same, comb, 0.0), axis=0, keepdims=True)
            comb_out[i, k] = jnp.broadcast_to(row, comb_out.shape[2:])
            scaled[i, k] = (factor * hidden).astype(BF)
            weighted = factor * part
            slope = up * logistic * (1.0 + gate * (1.0 - logistic))
            grad[i, k, :, pl.ds(0, ff)] = (weighted * slope).astype(BF)
            grad[i, k, :, pl.ds(ff, ff)] = (weighted * active).astype(BF)

    def sem(c, half, i):
        return back_send.at[c, half, i], back_recv.at[c, half, i]

    waits = {}

    def tiles(half, c, pieces):
        u, v = uv[half]
        cols = pl.ds(*CHUNKS[c])
        rows = []
        for j, first, last, _ in pieces:
            for k in range(first, last):
                rows.append(grad[PLACE[j], k] if half == 0 else grad[k, PLACE[j]])
        out = contract(jnp.concatenate(rows, axis=0), wgu[half, cols, :], 1, 1).astype(BF)
        n = 0
        for j, first, last, number in pieces:
            span = last - first
            part = out[n * SLOT : (n + span) * SLOT].reshape(span, SLOT, -1)
            n += span
            if j == 0:
                returned[half, pl.ds(first, span), 0, :, cols] = part
                continue
            outgoing[half, j - 1, pl.ds(first, span), :, cols] = part
            copy = remote(
                outgoing.at[half, j - 1, pl.ds(first, span), :, cols],
                returned.at[half, pl.ds(first, span), PLACE[SIDE - j], :, cols],
                *sem(c, half, number),
                expert=at(half, u, mod4(v + j)),
            )
            go(copy)
            waits.setdefault((half, c), []).append(copy)

    def turn(half, c):
        u, v = uv[half]
        start, size = CHUNKS[c]
        cols = pl.ds(start, size)
        up, down = at(half, mod4(u + 1), v), at(half, mod4(u + 3), v)
        for copy in waits[(half, c)]:
            copy.wait_recv()
        for o in (2, 1, 3, 0):
            source = at(half, mod4(u + o), v)
            maps = jnp.concatenate(
                [one_hot(slots_of(source, at(half, u, mod4(v + w)))) for w in ORDER], axis=0
            )
            total = contract(maps, returned[half, PLACE[o], :, :, cols].reshape(group, size), 0, 0)
            if o == 2:
                sending[half, 0, :, cols] = total.astype(BF)
                go(remote(sending.at[half, 0, LOW, cols], half_in.at[half, 0, :, cols], *sem(c, half, 5), expert=up))
                go(remote(sending.at[half, 0, HIGH, cols], half_in.at[half, 1, :, cols], *sem(c, half, 6), expert=down))
            else:
                partial[half, (2 + c % 2, 0, 2, 1)[o], :, pl.ds(0, size)] = total

    def add_up(half, c):
        u, v = uv[half]
        start, size = CHUNKS[c]
        cols = pl.ds(start, size)
        up, down = at(half, mod4(u + 1), v), at(half, mod4(u + 3), v)
        for d, to, met, other in ((0, up, LOW, HIGH), (1, down, HIGH, LOW)):
            piece = half_in.at[half, d, :, cols]
            remote(piece, piece, *sem(c, half, 5 + d), expert=to).wait_recv()
            sending[half, 1 + d, met, cols] = (
                partial[half, d, met, pl.ds(0, size)] + half_in[half, d, :, cols].astype(F32)
            ).astype(BF)
            sending[half, 1 + d, other, cols] = partial[half, d, other, pl.ds(0, size)].astype(BF)
            go(remote(sending.at[half, 1 + d, :, cols], full_in.at[half, d, :, cols], *sem(c, half, 7 + d), expert=to))

    def finish(half, c):
        u, v = uv[half]
        start, size = CHUNKS[c]
        cols = pl.ds(start, size)
        for d, to in ((0, at(half, mod4(u + 1), v)), (1, at(half, mod4(u + 3), v))):
            piece = full_in.at[half, d, :, cols]
            remote(piece, piece, *sem(c, half, 7 + d), expert=to).wait_recv()
        total = partial[half, 2 + c % 2, :, pl.ds(0, size)] + (
            full_in[half, 0, :, cols].astype(F32) + full_in[half, 1, :, cols].astype(F32)
        )
        place = pl.ds(half * width + start, size)
        final[:, place] = total.astype(BF)
        go(remote(final.at[:, place], passed.at[:, place], *sem(c, half, 9), pipe=mod4(pipe + 3)))

    gu_count = width // GU_STEP
    busy = {}
    others = {}

    def free(key):
        if key in busy:
            copy, away = busy.pop(key)
            copy.wait_send() if away else copy.wait()

    def fetch(kind, i):
        n = i if kind == "gu" else gu_count + i
        ref, other = (gu_part, gu_other) if kind == "gu" else (dn_part, dn_other)
        rows = pl.ds(i * GU_STEP, GU_STEP) if kind == "gu" else pl.ds(*DN_CUTS[i])
        piece = ref.at[rows]
        remote(piece, piece, dw_send.at[n], dw_recv.at[n], dp=1 - dp).wait_recv()
        copy = pltpu.make_async_copy(piece, other.at[pl.ds(0, rows.size)], other_sem.at[n])
        copy.start()
        others[(kind, i)] = copy

    def grad_unit(kind, away, i):
        side = 1 - dp if away else dp
        if kind == "gu":
            count, n, rows = gu_count, i, pl.ds(i * GU_STEP, GU_STEP)
            cols = pl.ds(pl.multiple_of(side * width + i * GU_STEP, GU_STEP), GU_STEP)
            left = saved[:, :, :, cols].reshape(SIDE * group, GU_STEP)
            right = grad[...].reshape(SIDE * group, 2 * ff)
            stage, part, own, other = gu_stage, gu_part, gu_grad, gu_other
        else:
            count, n, rows = len(DN_CUTS), gu_count + i, pl.ds(*DN_CUTS[i])
            left = scaled[:, :, :, rows].reshape(SIDE * group, rows.size)
            right = dy[pl.ds(side, 1)].reshape(SIDE * group, width)
            stage, part, own, other = dn_stage, dn_part, dn_grad, dn_other
        turn_no = (0 if away else count) + i
        key = (kind, turn_no % 2)
        out = contract(left, right, 0, 0)
        free(key)
        slot = stage.at[turn_no % 2, pl.ds(0, rows.size)]
        if away:
            slot[...] = out.astype(BF)
            copy = remote(slot, part.at[rows], dw_send.at[n], dw_recv.at[n], dp=1 - dp)
        else:
            others.pop((kind, i)).wait()
            slot[...] = (out + other[pl.ds(0, rows.size), :].astype(F32)).astype(BF)
            if i + 1 < count:
                fetch(kind, i + 1)
            copy = pltpu.make_async_copy(slot, own.at[rows], own_sem.at[n])
        copy.start()
        busy[key] = (copy, away)

    units = [functools.partial(grad_unit, "dn", True, i) for i in range(len(DN_CUTS))]
    units += [functools.partial(grad_unit, "gu", True, i) for i in range(gu_count)]
    units += [functools.partial(fetch, "dn", 0), functools.partial(fetch, "gu", 0)]
    units += [functools.partial(grad_unit, "dn", False, i) for i in range(len(DN_CUTS))]
    units += [functools.partial(grad_unit, "gu", False, i) for i in range(gu_count)]

    def work(count):
        for _ in range(min(count, len(units))):
            units.pop(0)()

    for half in BOTH:
        deliver(half, 0)
    for copy in row_tables:
        copy.wait_recv()
    mine = pl.ds(y * SIDE, SIDE)
    col_tables = [
        remote(table.at[mine], table.at[mine], table_send.at[3 + i], table_recv.at[3 + i], expert=col_peers[i])
        for i in range(3)
    ]
    for copy in col_tables:
        go(copy)
    for half in BOTH:
        for copy in near[half]:
            copy.wait_recv()
        for copy in ring(half, 1):
            go(copy)
    for copy in col_tables:
        copy.wait_recv()
    for r in (1, 2):
        for half in BOTH:
            deliver(half, r)
    for half in BOTH:
        for copy in ring(half, 1):
            copy.wait_recv()
        deliver(half, 3)
    across[0].wait_recv()
    through_rows([(0, 0)])
    through_rows([(0, 1), (1, 0), (1, 1)])
    through_rows([(0, 2), (2, 0), (1, 2), (2, 1), (2, 2)])
    across[1].wait_recv()
    need("wgu")
    for c in range(len(CHUNKS)):
        for half in BOTH:
            tiles(half, c, ((1, 0, 3, 0), (3, 0, 3, 1), (0, 0, 3, None)))
    through_rows([(0, 3), (3, 0), (1, 3), (3, 1)])
    through_rows([(2, 3), (3, 2), (3, 3)])
    comb_cols = [
        remote(
            comb_out.at[PLACE[i]], comb_mid.at[PLACE[SIDE - i]],
            comb_send.at[i - 1], comb_recv.at[i - 1], expert=col_peers[i - 1],
        )
        for i in (1, 2, 3)
    ]
    comb_rows = [
        remote(
            comb_mid.at[:, PLACE[i]], comb_in.at[PLACE[SIDE - i]],
            comb_send.at[2 + i], comb_recv.at[2 + i], expert=row_peers[i - 1],
        )
        for i in (1, 2, 3)
    ]
    comb_mid[0] = comb_out[0]
    for copy in comb_cols:
        go(copy)
    for c in range(len(CHUNKS)):
        for half in BOTH:
            tiles(half, c, ((2, 0, 4, 2), (1, 3, 4, 3), (3, 3, 4, 4), (0, 3, 4, None)))
    for copy in comb_cols:
        copy.wait_recv()
    for copy in comb_rows:
        go(copy)
    comb_in[0] = comb_mid[:, 0]
    need(*[("saved", i, k) for i in range(SIDE) for k in range(SIDE)])
    steps = {"turn": turn, "add": add_up, "finish": finish}
    for count, step, c in STEPS:
        work(count)
        for half in BOTH:
            steps[step](half, c)
    work(len(units))
    for copy in comb_rows:
        copy.wait_recv()
    for k in range(TOP):
        total = jnp.zeros((1, TOK), F32)
        for i in range(SIDE):
            for j in range(SIDE):
                expert = mod4(y + ORDER[i]) * SIDE + mod4(x + ORDER[j])
                hit = picks[pl.ds(k, 1), :] == expert.astype(F32)
                total = total + jnp.where(hit, comb_in[j, i, pl.ds(0, 1), :], 0.0)
        comb_grad[pl.ds(k, 1), :] = total
    for key in list(busy):
        free(key)
    for c, (start, size) in enumerate(CHUNKS):
        for half in BOTH:
            place = pl.ds(half * width + start, size)
            piece = passed.at[:, place]
            remote(piece, piece, *sem(c, half, 9), pipe=mod4(pipe + 3)).wait_recv()
    for copy in sends:
        copy.wait_send()


def layer(tok, picks, wgu, wdn, inputs, gate_up):
    width, both = wgu.shape
    ff = both // 2
    vmem = pl.BlockSpec(memory_space=pltpu.VMEM)
    hbm = pl.BlockSpec(memory_space=pltpu.HBM)
    widest = max(size for _, size in CHUNKS)
    cut = max(size for _, size in DN_CUTS)
    count = width // GU_STEP + len(DN_CUTS)
    dma = pltpu.SemaphoreType.DMA
    return pl.pallas_call(
        layer_kernel,
        out_shape=(
            jax.ShapeDtypeStruct((TOK, 2 * width), BF),
            jax.ShapeDtypeStruct((TOP, TOK), F32),
            jax.ShapeDtypeStruct(wgu.shape, BF),
            jax.ShapeDtypeStruct(wdn.shape, BF),
            jax.ShapeDtypeStruct(wgu.shape, BF),
            jax.ShapeDtypeStruct(wdn.shape, BF),
        ),
        in_specs=[vmem, vmem, hbm, hbm, hbm, hbm],
        out_specs=(hbm, vmem, hbm, hbm, hbm, hbm),
        scratch_shapes=[
            pltpu.VMEM((2,) + wgu.shape, BF),
            pltpu.VMEM((2,) + wdn.shape, BF),
            pltpu.VMEM((2, SIDE, SIDE, SLOT, width), BF),
            pltpu.VMEM((SIDE, SIDE, SLOT, 2 * width), BF),
            pltpu.VMEM((SIDE, SIDE, SLOT, both), BF),
            pltpu.VMEM((SIDE, SIDE, SLOT, ff), BF),
            pltpu.VMEM((EXPERTS, 2 * EXPERTS, TOK), F32),
            pltpu.VMEM((2, 3, TOK, width), BF),
            pltpu.VMEM((2, 3, SIDE, SLOT, width), BF),
            pltpu.VMEM((2, 3, SIDE, SLOT, width), BF),
            pltpu.VMEM((2, SIDE, SIDE, SLOT, width), BF),
            pltpu.VMEM((2, 4, TOK, widest), F32),
            pltpu.VMEM((2, 3, TOK, width), BF),
            pltpu.VMEM((2, 2, TOK // 2, width), BF),
            pltpu.VMEM((2, 2, TOK, width), BF),
            pltpu.VMEM((TOK, 2 * width), BF),
            pltpu.VMEM((SIDE, SIDE, 8, TOK), F32),
            pltpu.VMEM((SIDE, SIDE, 8, TOK), F32),
            pltpu.VMEM((SIDE, SIDE, 8, TOK), F32),
            pltpu.VMEM((2, GU_STEP, both), BF),
            pltpu.VMEM((2, cut, width), BF),
            pltpu.VMEM((GU_STEP, both), BF),
            pltpu.VMEM((cut, width), BF),
            dma((2,)),
            dma((SIDE, SIDE)),
            dma((SIDE, SIDE)),
            dma((2, 4)),
            dma((2, 4)),
            dma((2, SIDE, 3)),
            dma((2, SIDE, 3)),
            dma((6,)),
            dma((6,)),
            dma((2,)),
            dma((2,)),
            dma((len(CHUNKS), 2, 10)),
            dma((len(CHUNKS), 2, 10)),
            dma((6,)),
            dma((6,)),
            dma((count,)),
            dma((count,)),
            dma((count,)),
            dma((count,)),
        ],
        compiler_params=pltpu.CompilerParams(
            collective_id=0, has_side_effects=True, vmem_limit_bytes=64 * 1024 * 1024
        ),
        name="layer",
    )(tok, picks, wgu, wdn, inputs, gate_up)


def keep_kernel(*refs):
    n = len(KEEP)
    sources, kept, held = refs[:n], refs[n : 2 * n], refs[2 * n : 3 * n]
    sem_in, sem_out = refs[3 * n :]
    pieces = [(i, part) for i in range(n) for part in range(KEEP[i])]

    def rows(i, part):
        size = sources[i].shape[0] // KEEP[i]
        return pl.ds(part * size, size)

    ins = [
        pltpu.make_async_copy(sources[i].at[rows(i, part)], held[i].at[rows(i, part)], sem_in.at[i, part])
        for i, part in pieces
    ]
    outs = [
        pltpu.make_async_copy(held[i].at[rows(i, part)], kept[i].at[rows(i, part)], sem_out.at[i, part])
        for i, part in pieces
    ]
    for copy in ins:
        copy.start()
    for copy, out in zip(ins, outs):
        copy.wait()
        out.start()
    for out in outs:
        out.wait()


def keep(*arrays):
    hbm = pl.BlockSpec(memory_space=pltpu.HBM)
    return pl.pallas_call(
        keep_kernel,
        out_shape=tuple(jax.ShapeDtypeStruct(a.shape, a.dtype) for a in arrays),
        in_specs=[hbm] * len(arrays),
        out_specs=(hbm,) * len(arrays),
        scratch_shapes=[pltpu.VMEM(a.shape, a.dtype) for a in arrays]
        + [pltpu.SemaphoreType.DMA((len(arrays), max(KEEP)))] * 2,
        compiler_params=pltpu.CompilerParams(vmem_limit_bytes=60 * 1024 * 1024),
        name="keep",
    )(*arrays)


def body(out_grad, routes, combine, gate_up_weight, down_weight, saved_inputs, saved_gate_up):
    picks = jnp.concatenate([routes[0].T.astype(F32), combine[0].T.astype(F32)], axis=0)
    passed, comb, gu_grad, dn_grad, _, _ = layer(
        out_grad[0], picks, gate_up_weight[0, 0], down_weight[0, 0], saved_inputs[0, 0, 0], saved_gate_up[0, 0, 0]
    )
    passed, gu_grad, dn_grad = keep(passed, gu_grad, dn_grad)
    return passed[None], comb.T.astype(BF)[None], gu_grad[None, None], dn_grad[None, None]


def solution(mesh):
    placed = (
        P("pipe", ("dp", "expert"), None),
        P("pipe", ("dp", "expert"), None),
        P("pipe", ("dp", "expert"), None),
        P("pipe", "expert", "dp", None),
        P("pipe", "expert", None, "dp"),
        P("pipe", "dp", "expert", None, None),
        P("pipe", "dp", "expert", None, None),
    )
    return jax.shard_map(
        body,
        mesh=mesh,
        in_specs=placed,
        out_specs=(
            P("pipe", ("dp", "expert"), None),
            P("pipe", ("dp", "expert"), None),
            P("pipe", "expert", "dp", None),
            P("pipe", "expert", None, "dp"),
        ),
        check_vma=False,
    )
```
